128 devices in a mesh: cam: 32 (over y, x, core), lidar: 4 (over z).
Axes of the slice: x: 4, y: 4, z: 4, core: 2. Of those that a mesh axis runs over, the one named last changes fastest.
Arguments:
- key_feats: bfloat16 [8192, 128, 256], P(('cam', 'lidar')), may hold values from -6 to 6
- query_feats: bfloat16 [512, 128, 256], P(('cam', 'lidar')), may hold values from -6 to 6
- key_dest: int32 [8192], P(('cam', 'lidar')), may hold values from 0 to 127, as said below
- key_scene: int32 [8192], P(('cam', 'lidar')), may hold values from 0 to 3
- key_count: int32 [8192], P(('cam', 'lidar')), may hold values from 16 to 128, as said below
- pos_tile: int32 [512], P(('cam', 'lidar')), may hold values from 0 to 8191, as said below
- pos_row: int32 [512, 128], P(('cam', 'lidar')), may hold values from 0 to 127, as said below
Outputs:
- query_loss: float32 [512, 128], P(('cam', 'lidar'))
- key_grad: bfloat16 [8192, 128, 256], P(('cam', 'lidar'))
The draws below stay inside these ranges and needn't reach their ends.
Inputs may be any that keep to these rules, and one draw needn't show every extreme that they name: `key_dest`: the 64 key tiles of one device go to 64 different devices; each device gets a tile from the device with index one lower (cyclically), and one device gets a tile from every device. `key_count`: the first key tile of each device is full. pos_tile[i] is a key tile with key_dest equal to the owner of query tile i; a query tile takes its scene from that key tile, so tiles of one device may share a scene. pos_row[i, r] < key_count[pos_tile[i]].
All inputs are finite; a program needn't handle non-finite values.
Results may differ from the reference program's by a relative error of at most 0.0053.
Values may be sent and summed in bfloat16 or wider, within the bound.
No kernel may reach another device: no remote copies, remote signals or barrier semaphores. Data moves between devices by JAX's collectives and lax.ppermute only.
A program may use at most 192 MiB of HBM per device.

```python
import math
import jax
import jax.numpy as jnp
from jax import lax

E = 256
TILE = 128
QT_DEV = 4
SC_DEV = 4
KT_DEV = 64
KTILES = 8192
QTILES = 512
DEVICES = 128


def route_table(key):
    base = jax.random.fold_in(key, 101)
    key_weight, key_noise, key_hot, key_order = jax.random.split(base, 4)
    weight = jax.random.randint(key_weight, (DEVICES,), 1, 5)
    noise = jax.random.randint(key_noise, (DEVICES, DEVICES), 0, 4096)
    score = noise * weight[None, :]
    hot = jax.random.randint(key_hot, (), 0, DEVICES)
    source = jnp.arange(DEVICES, dtype=jnp.int32)[:, None]
    target = jnp.arange(DEVICES, dtype=jnp.int32)[None, :]
    score = jnp.where(target == hot, 40000, score)
    score = jnp.where(target == (source + 1) % DEVICES, 50000, score)
    score = score * DEVICES + target
    unused, chosen = lax.top_k(score, KT_DEV)
    order_keys = jax.random.split(key_order, DEVICES)
    order = jax.vmap(lambda one: jax.random.permutation(one, KT_DEV))(order_keys)
    chosen = jnp.take_along_axis(chosen, order, axis=1)
    return chosen.reshape(-1).astype(jnp.int32)


def count_table(key):
    base = jax.random.fold_in(key, 102)
    counts = jax.random.randint(base, (KTILES,), TILE // 8, TILE + 1)
    counts = counts.at[::KT_DEV].set(TILE)
    return counts.astype(jnp.int32)


def pick_tiles(key):
    dest = route_table(key)
    base = jax.random.fold_in(key, 103)
    rank = jax.random.permutation(base, KTILES).astype(jnp.int32)
    owner = jnp.arange(QTILES, dtype=jnp.int32) // QT_DEV
    match = dest[None, :] == owner[:, None]
    score = jnp.where(match, rank[None, :] + KTILES, rank[None, :])
    return jnp.argmax(score, axis=1).astype(jnp.int32)


def draw_key_dest(key, part):
    return route_table(key)


def draw_key_count(key, part):
    return count_table(key)


def draw_pos_tile(key, part):
    return pick_tiles(key)


def draw_pos_row(key, part):
    tiles = pick_tiles(key)
    counts = count_table(key)
    own = jax.random.fold_in(key, 9)
    raw = jax.random.randint(own, (QTILES, TILE), 0, 1 << 20)
    return (raw % counts[tiles][:, None]).astype(jnp.int32)


def place_ends(drawn, stream_key, least, high):
    longest = drawn.shape.index(max(drawn.shape))
    spots = []
    for shift in (0, 1):
        where = [jax.random.randint(jax.random.fold_in(stream_key, axis), (), 0, length) for axis, length in enumerate(drawn.shape)]
        where[longest] = (where[longest] + shift) % drawn.shape[longest]
        spots.append(tuple(where))
    return drawn.at[spots[0]].set(least).at[spots[1]].set(high)


def levels(own_key, extent, shards, low, high):
    gain, own = 1.0, jax.random.fold_in(own_key, 6)
    for axis_at, parts in shards:
        heights = jnp.exp(jax.random.uniform(jax.random.fold_in(own, axis_at), (parts,), jnp.float32, low / len(shards), high / len(shards)))
        gain = gain * jnp.repeat(heights, extent[axis_at] // parts).reshape([-1 if axis == axis_at else 1 for axis in range(len(extent))])
    return gain


def centred(own_key, extent, scale, limit, cuts=(), kind=jnp.bfloat16):
    drawn = jax.random.normal(own_key, extent, jnp.float32) * scale
    if len(cuts) > 0:
        drawn = levels(own_key, extent, cuts, -0.22, 0.18) * drawn
    return jnp.clip(drawn, min=-limit, max=limit).astype(kind)


def setup_inputs(seed: int = 0) -> dict:
    key_list = jax.random.split(jax.random.key(seed), 8)
    key_feats = centred(key_list[0], (KTILES, TILE, E), 1.0, 6.0, ((0, 128),))
    query_feats = centred(key_list[1], (QTILES, TILE, E), 1.0, 6.0, ((0, 128),))
    key_dest = draw_key_dest(jax.random.fold_in(key_list[7], 71), 0)
    key_scene = place_ends(jax.random.randint(key_list[3], (KTILES,), 0, SC_DEV), jax.random.fold_in(key_list[3], 1), 0, SC_DEV - 1).astype(jnp.int32)
    key_count = draw_key_count(jax.random.fold_in(key_list[7], 71), 0)
    pos_tile = draw_pos_tile(jax.random.fold_in(key_list[7], 71), 0)
    pos_row = draw_pos_row(jax.random.fold_in(key_list[7], 71), 0)
    return dict(key_feats=key_feats, query_feats=query_feats, key_dest=key_dest, key_scene=key_scene, key_count=key_count, pos_tile=pos_tile, pos_row=pos_row)


inv_temp = 1.0 / 0.07
eps = 1e-06

def unit_rows(x):
    xf = x.astype(jnp.float32)
    scaled = xf * lax.rsqrt(lax.optimization_barrier(jnp.mean(xf * xf, axis=-1, keepdims=True)) + eps) / math.sqrt(x.shape[-1])
    return scaled.astype(jnp.bfloat16)

def reference(key_feats, query_feats, key_dest, key_scene, key_count, pos_tile, pos_row):
    normed_keys = unit_rows(key_feats)
    normed_queries = unit_rows(query_feats)
    tile_index = jnp.arange(KTILES, dtype=jnp.int32)
    source = tile_index // KT_DEV
    table = jnp.full((DEVICES, DEVICES), KTILES, jnp.int32).at[key_dest, source].set(tile_index)
    filled = table < KTILES
    safe = jnp.minimum(table, KTILES - 1)
    row_iota = jnp.arange(TILE, dtype=jnp.int32)
    column_iota = jnp.arange(DEVICES * TILE, dtype=jnp.int32)

    def one_device(grads, device):
        slots = safe[device]
        counts = jnp.where(filled[device], key_count[slots], 0)
        keys = normed_keys[slots].reshape(DEVICES * TILE, E)
        key_ok = (row_iota[None, :] < counts[:, None]).reshape(-1)
        scenes = jnp.repeat(key_scene[slots], TILE)
        start = (device * QT_DEV).astype(jnp.int32)
        queries = lax.dynamic_slice_in_dim(normed_queries, start, QT_DEV, 0).reshape(QT_DEV * TILE, E)
        targets = lax.dynamic_slice_in_dim(pos_tile, start, QT_DEV, 0)
        rows = lax.dynamic_slice_in_dim(pos_row, start, QT_DEV, 0)
        q_scene = jnp.repeat(key_scene[targets], TILE)
        column = ((targets // KT_DEV)[:, None] * TILE + rows).reshape(-1)
        logits = jnp.dot(queries, keys.T, preferred_element_type=jnp.float32) * inv_temp
        allowed = key_ok[None, :] & (scenes[None, :] == q_scene[:, None])
        expo = jnp.where(allowed, jnp.exp(logits), 0.0)
        total = lax.optimization_barrier(jnp.sum(expo, axis=1))
        picked = jnp.take_along_axis(logits, column[:, None], axis=1)[:, 0]
        loss = jnp.log(total) - picked
        target = (column_iota[None, :] == column[:, None]).astype(jnp.float32)
        weights = (expo / total[:, None] - target).astype(jnp.bfloat16)
        grad = jnp.dot(weights.T, queries, preferred_element_type=jnp.float32) * inv_temp
        grad = grad.astype(jnp.bfloat16).reshape(DEVICES, TILE, E)
        grads = grads.at[table[device]].set(grad, mode='drop')
        return (grads, loss.reshape(QT_DEV, TILE))
    grads, losses = lax.scan(one_device, jnp.zeros((KTILES, TILE, E), jnp.bfloat16), jnp.arange(DEVICES, dtype=jnp.int32))
    return (losses.reshape(QTILES, TILE), grads)
```

```python
import math

import jax
import jax.numpy as jnp
from jax import lax
from jax.experimental import pallas as pl
from jax.experimental.pallas import tpu as pltpu
from jax.sharding import PartitionSpec as P

inv_temp = 1.0 / 0.07
log2_scale = inv_temp * math.log2(math.e)
eps = 1e-06
GROUP = 4
AXES = ("cam", "lidar")


def unit_rows(x):
    xf = x.astype(jnp.float32)
    scaled = (
        xf * lax.rsqrt(jnp.mean(xf * xf, axis=-1, keepdims=True) + eps) / math.sqrt(x.shape[-1])
    )
    return scaled.astype(jnp.bfloat16)


def exchange(x):
    return lax.all_to_all(x, AXES, split_axis=0, concat_axis=0, tiled=True)


def products(keys, queries):
    return lax.dot_general(
        keys, queries, (((1,), (1,)), ((), ())), preferred_element_type=jnp.float32
    )


def total_kernel(dest, count, nk_ref, *rest):
    q_refs, code_ref, out_ref = rest[:GROUP], rest[GROUP], rest[GROUP + 1]
    rows = nk_ref.shape[1]
    lanes = code_ref.shape[2]
    step = pl.program_id(0)

    @pl.when(step == 0)
    def _():
        out_ref[...] = jnp.zeros_like(out_ref)

    row = lax.broadcasted_iota(jnp.int32, (rows, lanes), 0)
    for j in range(GROUP):
        tile = step * GROUP + j
        owner = dest[tile]
        live = row < count[tile]
        raw = products(nk_ref[j], q_refs[j][0])
        codes = code_ref[owner]
        totals, picks = [], []
        for i in range(codes.shape[0]):
            part = raw[:, i * lanes : (i + 1) * lanes]
            code = codes[i : i + 1, :]
            expo = jnp.where(live, jnp.exp2(part * log2_scale), 0.0)
            total = jnp.sum(expo, axis=0, keepdims=True)
            totals.append(jnp.where(code > -2, total, 0.0))
            picked = jnp.sum(jnp.where(row == code, part, 0.0), axis=0, keepdims=True)
            picks.append(picked * inv_temp)
        out_ref[owner] = jnp.concatenate(totals + picks, axis=0)


def grad_kernel(dest, count, nk_ref, *rest):
    q_refs, code_ref, scale_ref, out_ref = (
        rest[:GROUP],
        rest[GROUP],
        rest[GROUP + 1],
        rest[GROUP + 2],
    )
    rows = nk_ref.shape[1]
    lanes = code_ref.shape[2]
    step = pl.program_id(0)
    row = lax.broadcasted_iota(jnp.int32, (rows, lanes), 0)
    for j in range(GROUP):
        tile = step * GROUP + j
        owner = dest[tile]
        live = row < count[tile]
        raw = products(nk_ref[j], q_refs[j][0])
        codes = code_ref[owner]
        scales = jnp.where(codes > -2, scale_ref[owner], 0.0)
        weights = []
        for i in range(codes.shape[0]):
            part = raw[:, i * lanes : (i + 1) * lanes]
            expo = jnp.where(live, jnp.exp2(part * log2_scale), 0.0)
            target = jnp.where(row == codes[i : i + 1, :], 1.0, 0.0)
            weights.append((expo * scales[i : i + 1, :] - target).astype(jnp.bfloat16))
        grad = jnp.dot(
            jnp.concatenate(weights, axis=1), q_refs[j][0], preferred_element_type=jnp.float32
        )
        out_ref[j] = (grad * inv_temp).astype(jnp.bfloat16)


def query_spec(j, block):
    return pl.BlockSpec(block, lambda step, dest, count: (dest[step * GROUP + j], 0, 0))


def tile_call(kernel, dest, count, nk, queries, tables, out_shape, out_spec, name):
    tiles, rows, width = nk.shape
    devices, query_rows, _ = queries.shape
    key_spec = pl.BlockSpec((GROUP, rows, width), lambda step, dest, count: (step, 0, 0))
    table_specs = [
        pl.BlockSpec(t.shape, lambda step, dest, count: (0, 0, 0)) for t in tables
    ]
    return pl.pallas_call(
        kernel,
        grid_spec=pltpu.PrefetchScalarGridSpec(
            num_scalar_prefetch=2,
            grid=(tiles // GROUP,),
            in_specs=[key_spec]
            + [query_spec(j, (1, query_rows, width)) for j in range(GROUP)]
            + table_specs,
            out_specs=out_spec,
        ),
        out_shape=out_shape,
        compiler_params=pltpu.CompilerParams(vmem_limit_bytes=48 * 1024 * 1024),
        name=name,
    )(dest, count, nk, *([queries] * GROUP), *tables)


def shards(key_feats, query_feats, key_dest, key_scene, key_count, pos_tile, pos_row):
    tiles, rows, width = key_feats.shape
    query_tiles = query_feats.shape[0]
    devices = lax.axis_size("cam") * lax.axis_size("lidar")
    normq = unit_rows(query_feats).reshape(1, query_tiles * rows, width)
    queries = lax.all_gather(normq, AXES, axis=0, tiled=True)

    device_iota = jnp.arange(devices, dtype=jnp.int32)
    owned = key_dest[None, :] == device_iota[:, None]
    scene_out = jnp.sum(jnp.where(owned, key_scene[None, :] + 1, 0), axis=1)
    scene_in = exchange(scene_out.reshape(devices, 1, 1)).reshape(devices)
    pos_source = pos_tile // tiles
    hit = pos_source[None, :] == device_iota[:, None]
    query_scene = jnp.sum(jnp.where(hit, scene_in[:, None], 0), axis=0)
    same = scene_in[:, None] == query_scene[None, :]
    code = jnp.where(
        hit[:, :, None], pos_row[None, :, :], jnp.where(same[:, :, None], -1, -2)
    )
    code = exchange(code)

    nk = unit_rows(key_feats)
    step_block = lambda step, dest, count: (step, 0, 0)
    whole = lambda step, dest, count: (0, 0, 0)
    partial = tile_call(
        total_kernel,
        key_dest,
        key_count,
        nk,
        queries,
        [code],
        jax.ShapeDtypeStruct((devices, 2 * query_tiles, rows), jnp.float32),
        pl.BlockSpec((devices, 2 * query_tiles, rows), whole),
        "totals",
    )
    arrived = jnp.sum(exchange(partial), axis=0)
    total, picked = arrived[:query_tiles], arrived[query_tiles:]
    scale = exchange(jnp.broadcast_to((1.0 / total)[None], (devices, query_tiles, rows)))
    loss = jnp.log(total) - picked
    key_grad = tile_call(
        grad_kernel,
        key_dest,
        key_count,
        nk,
        queries,
        [code, scale],
        jax.ShapeDtypeStruct((tiles, rows, width), jnp.bfloat16),
        pl.BlockSpec((GROUP, rows, width), step_block),
        "grads",
    )
    return (loss, key_grad)


def solution(mesh):
    return jax.shard_map(
        shards,
        mesh=mesh,
        in_specs=(
            P(AXES, None, None),
            P(AXES, None, None),
            P(AXES),
            P(AXES),
            P(AXES),
            P(AXES),
            P(AXES, None),
        ),
        out_specs=(P(AXES, None), P(AXES, None, None)),
        check_vma=False,
    )
```

```python
import functools
import math

import jax
import jax.numpy as jnp
from jax import lax
from jax.experimental import pallas as pl
from jax.experimental.pallas import tpu as pltpu
from jax.sharding import PartitionSpec as P

inv_temp = 1.0 / 0.07
log2_scale = inv_temp * math.log2(math.e)
eps = 1e-06
GROUP = 8
AHEAD = 3
AXES = ("cam", "lidar")


def unit_rows(x):
    xf = x.astype(jnp.float32)
    scaled = (
        xf * lax.rsqrt(jnp.mean(xf * xf, axis=-1, keepdims=True) + eps) / math.sqrt(x.shape[-1])
    )
    return scaled.astype(jnp.bfloat16)


def exchange(x):
    return lax.all_to_all(x, AXES, split_axis=0, concat_axis=0, tiled=True)


def products(keys, queries):
    return lax.dot_general(
        keys, queries, (((1,), (1,)), ((), ())), preferred_element_type=jnp.float32
    )


def fetcher(pair_query, nk_hbm, q_hbm, nk_buf, q_buf, nk_sem, q_sem):
    pltpu.make_async_copy(nk_hbm, nk_buf, nk_sem).start()

    def fetch(group, act):
        for j in range(GROUP):
            p = group * GROUP + j
            copy = pltpu.make_async_copy(q_hbm.at[pair_query[p]], q_buf.at[p], q_sem.at[p])
            act(copy)

    return fetch


def over_groups(pairs, fetch, first, body):
    groups = (pairs + (GROUP - 1)) // GROUP
    start = lambda copy: copy.start()
    for ahead in range(AHEAD):

        @pl.when(ahead < groups)
        def _():
            fetch(ahead, start)

    first()

    @pl.loop(0, groups)
    def _(group):
        @pl.when(group + AHEAD < groups)
        def _():
            fetch(group + AHEAD, start)

        fetch(group, lambda copy: copy.wait())
        for j in range(GROUP):
            body(group * GROUP + j)


def total_kernel(
    slots, pair_tile, pair_query, pair_out, pairs, count, nk_hbm, q_hbm, code_ref, out_ref,
    nk_buf, q_buf, nk_sem, q_sem,
):
    rows = nk_buf.shape[1]
    row = lax.broadcasted_iota(jnp.int32, (rows, code_ref.shape[1]), 0)
    fetch = fetcher(pair_query, nk_hbm, q_hbm, nk_buf, q_buf, nk_sem, q_sem)

    def first():
        out_ref[...] = jnp.zeros_like(out_ref)
        pltpu.make_async_copy(nk_hbm, nk_buf, nk_sem).wait()

    def body(p):
        tile = pair_tile[p]
        raw = products(nk_buf[tile], q_buf[p])
        code = code_ref[pl.ds(pair_query[p], 1), :]
        expo = jnp.where(row < count[tile], jnp.exp2(raw * log2_scale), 0.0)
        total = jnp.sum(expo, axis=0, keepdims=True)
        picked = jnp.sum(jnp.where(row == code, raw, 0.0), axis=0, keepdims=True)
        out_ref[pl.ds(pair_out[p], 1), :] = jnp.where(code > -2, total, 0.0)
        out_ref[pl.ds(pair_out[p] + slots, 1), :] = picked * inv_temp

    over_groups(pairs[0], fetch, first, body)


def grad_kernel(
    pair_tile, pair_query, pairs, count, nk_hbm, q_hbm, code_ref, scale_ref, out_hbm,
    nk_buf, q_buf, sum_buf, out_buf, nk_sem, q_sem, out_sem,
):
    tiles, rows, width = nk_buf.shape
    row = lax.broadcasted_iota(jnp.int32, (rows, code_ref.shape[1]), 0)
    grad_row = lax.broadcasted_iota(jnp.int32, (rows, width), 0)
    fetch = fetcher(pair_query, nk_hbm, q_hbm, nk_buf, q_buf, nk_sem, q_sem)

    def first():
        sum_buf[...] = jnp.zeros_like(sum_buf)
        pltpu.make_async_copy(nk_hbm, nk_buf, nk_sem).wait()

    def body(p):
        tile, query = pair_tile[p], pair_query[p]
        raw = products(nk_buf[tile], q_buf[p])
        code = jnp.where(p < pairs[0], code_ref[pl.ds(query, 1), :], -2)
        scale = jnp.where(code > -2, scale_ref[pl.ds(query, 1), :], 0.0)
        target = jnp.where(row == code, 1.0, 0.0)
        weights = (jnp.exp2(raw * log2_scale) * scale - target).astype(jnp.bfloat16)
        sum_buf[tile] += jnp.dot(weights, q_buf[p], preferred_element_type=jnp.float32)

    over_groups(pairs[0], fetch, first, body)

    def part(group):
        span = pl.ds(group * GROUP, GROUP)
        return pltpu.make_async_copy(out_buf.at[span], out_hbm.at[span], out_sem.at[group])

    @pl.loop(0, tiles // GROUP)
    def _(group):
        for j in range(GROUP):
            tile = group * GROUP + j
            grad = jnp.where(grad_row < count[tile], sum_buf[tile] * inv_temp, 0.0)
            out_buf[tile] = grad.astype(jnp.bfloat16)
        part(group).start()

    @pl.loop(0, tiles // GROUP)
    def _(group):
        part(group).wait()


def tile_call(kernel, scalars, nk, queries, tables, out_shape, wide, name):
    tiles, rows, width = nk.shape
    most = scalars[0].shape[0]
    query_rows = queries.shape[1]
    smem, vmem, hbm = (pl.BlockSpec(memory_space=m) for m in (pltpu.SMEM, pltpu.VMEM, pl.ANY))
    buffers = [
        pltpu.VMEM((tiles, rows, width), jnp.bfloat16),
        pltpu.VMEM((most, query_rows, width), jnp.bfloat16),
    ]
    semaphores = [pltpu.SemaphoreType.DMA, pltpu.SemaphoreType.DMA((most,))]
    if wide:
        buffers += [
            pltpu.VMEM((tiles, rows, width), jnp.float32),
            pltpu.VMEM((tiles, rows, width), jnp.bfloat16),
        ]
        semaphores += [pltpu.SemaphoreType.DMA((tiles // GROUP,))]
    return pl.pallas_call(
        kernel,
        in_specs=[smem] * len(scalars) + [hbm, hbm] + [vmem] * len(tables),
        out_specs=hbm if wide else vmem,
        out_shape=out_shape,
        scratch_shapes=buffers + semaphores,
        compiler_params=pltpu.CompilerParams(vmem_limit_bytes=58 * 1024 * 1024),
        name=name,
    )(*scalars, nk, queries, *tables)


def pair_lists(code, key_dest, query_tiles):
    devices = code.shape[0]
    most = key_dest.shape[0] * query_tiles
    owned = key_dest[:, None] == jnp.arange(devices, dtype=jnp.int32)[None, :]
    allowed = (code[:, :, 0] > -2).astype(jnp.int32)
    match = jnp.sum(jnp.where(owned[:, :, None], allowed[None], 0), axis=1).reshape(most)
    index = jnp.arange(most, dtype=jnp.int32)
    place = jnp.sum(jnp.where(index[None, :] < index[:, None], match[None, :], 0), axis=1)
    tile = index // query_tiles
    slot = index % query_tiles
    owner = jnp.repeat(key_dest, query_tiles)
    chosen = (place[None, :] == index[:, None]) & (match[None, :] > 0)
    listed = lambda x: jnp.sum(jnp.where(chosen, x[None, :], 0), axis=1)
    pairs = jnp.sum(match)
    spare = index >= pairs
    pair_tile = listed(tile)
    pair_query = jnp.where(spare, owner[0] * query_tiles, listed(owner * query_tiles + slot))
    pair_out = jnp.where(
        spare, owner[0] * 2 * query_tiles, listed(owner * 2 * query_tiles + slot)
    )
    return pair_tile, pair_query, pair_out, pairs.reshape(1)


def shards(key_feats, query_feats, key_dest, key_scene, key_count, pos_tile, pos_row):
    tiles, rows, width = key_feats.shape
    query_tiles = query_feats.shape[0]
    devices = lax.axis_size("cam") * lax.axis_size("lidar")
    queries = lax.all_gather(unit_rows(query_feats), AXES, axis=0, tiled=True)

    device_iota = jnp.arange(devices, dtype=jnp.int32)
    owned = key_dest[None, :] == device_iota[:, None]
    scene_out = jnp.sum(jnp.where(owned, key_scene[None, :] + 1, 0), axis=1)
    scene_in = exchange(scene_out.reshape(devices, 1, 1)).reshape(devices)
    pos_source = pos_tile // tiles
    hit = pos_source[None, :] == device_iota[:, None]
    query_scene = jnp.sum(jnp.where(hit, scene_in[:, None], 0), axis=0)
    same = scene_in[:, None] == query_scene[None, :]
    code = jnp.where(
        hit[:, :, None], pos_row[None, :, :], jnp.where(same[:, :, None], -1, -2)
    )
    code = exchange(code)

    nk = unit_rows(key_feats)
    pair_tile, pair_query, pair_out, pairs = pair_lists(code, key_dest, query_tiles)
    code = code.reshape(devices * query_tiles, rows)
    partial = tile_call(
        functools.partial(total_kernel, query_tiles),
        [pair_tile, pair_query, pair_out, pairs, key_count],
        nk,
        queries,
        [code],
        jax.ShapeDtypeStruct((devices * 2 * query_tiles, rows), jnp.float32),
        False,
        "totals",
    )
    partial = partial.reshape(devices, 2 * query_tiles, rows)
    arrived = jnp.sum(exchange(partial), axis=0)
    total, picked = arrived[:query_tiles], arrived[query_tiles:]
    scale = exchange(jnp.broadcast_to((1.0 / total)[None], (devices, query_tiles, rows)))
    loss = jnp.log(total) - picked
    key_grad = tile_call(
        grad_kernel,
        [pair_tile, pair_query, pairs, key_count],
        nk,
        queries,
        [code, scale.reshape(devices * query_tiles, rows)],
        jax.ShapeDtypeStruct((tiles, rows, width), jnp.bfloat16),
        True,
        "grads",
    )
    return (loss, key_grad)


def solution(mesh):
    return jax.shard_map(
        shards,
        mesh=mesh,
        in_specs=(
            P(AXES, None, None),
            P(AXES, None, None),
            P(AXES),
            P(AXES),
            P(AXES),
            P(AXES),
            P(AXES, None),
        ),
        out_specs=(P(AXES, None), P(AXES, None, None)),
        check_vma=False,
    )
```

```python
import functools
import math

import jax
import jax.numpy as jnp
from jax import lax
from jax.experimental import pallas as pl
from jax.experimental.pallas import tpu as pltpu
from jax.sharding import PartitionSpec as P

inv_temp = 1.0 / 0.07
log2_scale = inv_temp * math.log2(math.e)
eps = 1e-06
TOTAL_GROUP = 8
GRAD_GROUP = 16
OUT_GROUP = 8
AXES = ("cam", "lidar")


def unit_rows(x):
    xf = x.astype(jnp.float32)
    scaled = (
        xf * lax.rsqrt(jnp.mean(xf * xf, axis=-1, keepdims=True) + eps) / math.sqrt(x.shape[-1])
    )
    return scaled.astype(jnp.bfloat16)


def exchange(x):
    return lax.all_to_all(x, AXES, split_axis=0, concat_axis=0, tiled=True)


def products(keys, queries):
    return lax.dot_general(
        keys, queries, (((1,), (1,)), ((), ())), preferred_element_type=jnp.float32
    )


def over_pairs(pairs, group, sources, first, body):
    slots = sources[0][2].shape[0]
    ahead = slots // group - 1
    groups = (pairs + (group - 1)) // group

    def fetch(step, act):
        base = lax.rem(step, ahead + 1) * group
        for j in range(group):
            for hbm, index, buf, sem in sources:
                copy = pltpu.make_async_copy(
                    hbm.at[index[step * group + j]], buf.at[base + j], sem.at[base + j]
                )
                act(copy)

    start = lambda copy: copy.start()
    for early in range(ahead):

        @pl.when(early < groups)
        def _():
            fetch(early, start)

    first()

    @pl.loop(0, groups)
    def _(step):
        @pl.when(step + ahead < groups)
        def _():
            fetch(step + ahead, start)

        fetch(step, lambda copy: copy.wait())
        base = lax.rem(step, ahead + 1) * group
        for j in range(group):
            body(step * group + j, base + j)


def total_kernel(
    slots, pair_tile, pair_query, pair_out, pairs, count, nk_hbm, q_hbm, code_ref, out_ref,
    nk_buf, q_buf, nk_sem, q_sem,
):
    row = lax.broadcasted_iota(jnp.int32, (nk_buf.shape[1], code_ref.shape[1]), 0)

    def first():
        out_ref[...] = jnp.zeros_like(out_ref)

    def body(p, slot):
        raw = products(nk_buf[slot], q_buf[slot])
        code = code_ref[pl.ds(pair_query[p], 1), :]
        expo = jnp.where(row < count[pair_tile[p]], jnp.exp2(raw * log2_scale), 0.0)
        total = jnp.sum(expo, axis=0, keepdims=True)
        picked = jnp.sum(jnp.where(row == code, raw, 0.0), axis=0, keepdims=True)
        out_ref[pl.ds(pair_out[p], 1), :] = jnp.where(code > -2, total, 0.0)
        out_ref[pl.ds(pair_out[p] + slots, 1), :] = picked * inv_temp

    sources = [(nk_hbm, pair_tile, nk_buf, nk_sem), (q_hbm, pair_query, q_buf, q_sem)]
    over_pairs(pairs[0], TOTAL_GROUP, sources, first, body)


def grad_kernel(
    pair_tile, pair_query, pairs, count, nk_hbm, q_hbm, code_ref, scale_ref, out_hbm,
    nk_buf, q_buf, nk_sem, q_sem, sum_buf, out_buf, out_sem,
):
    tiles, rows, width = sum_buf.shape
    row = lax.broadcasted_iota(jnp.int32, (rows, code_ref.shape[1]), 0)
    grad_row = lax.broadcasted_iota(jnp.int32, (rows, width), 0)

    def first():
        sum_buf[...] = jnp.zeros_like(sum_buf)

    def body(p, slot):
        tile, query = pair_tile[p], pair_query[p]
        raw = products(nk_buf[slot], q_buf[slot])
        code = jnp.where(p < pairs[0], code_ref[pl.ds(query, 1), :], -2)
        scale = jnp.where(code > -2, scale_ref[pl.ds(query, 1), :], 0.0)
        target = jnp.where(row == code, 1.0, 0.0)
        weights = (jnp.exp2(raw * log2_scale) * scale - target).astype(jnp.bfloat16)
        sum_buf[tile] += jnp.dot(weights, q_buf[slot], preferred_element_type=jnp.float32)

    sources = [(nk_hbm, pair_tile, nk_buf, nk_sem), (q_hbm, pair_query, q_buf, q_sem)]
    over_pairs(pairs[0], GRAD_GROUP, sources, first, body)

    def part(group):
        span = pl.ds(group * OUT_GROUP, OUT_GROUP)
        return pltpu.make_async_copy(out_buf.at[span], out_hbm.at[span], out_sem.at[group])

    @pl.loop(0, tiles // OUT_GROUP)
    def _(group):
        for j in range(OUT_GROUP):
            tile = group * OUT_GROUP + j
            grad = jnp.where(grad_row < count[tile], sum_buf[tile] * inv_temp, 0.0)
            out_buf[tile] = grad.astype(jnp.bfloat16)
        part(group).start()

    @pl.loop(0, tiles // OUT_GROUP)
    def _(group):
        part(group).wait()


def tile_call(kernel, scalars, nk, queries, tables, out_shape, slots, wide, name):
    tiles, rows, width = nk.shape
    smem, vmem, hbm = (pl.BlockSpec(memory_space=m) for m in (pltpu.SMEM, pltpu.VMEM, pl.ANY))
    scratch = [
        pltpu.VMEM((slots, rows, width), jnp.bfloat16),
        pltpu.VMEM((slots,) + queries.shape[1:], jnp.bfloat16),
        pltpu.SemaphoreType.DMA((slots,)),
        pltpu.SemaphoreType.DMA((slots,)),
    ]
    if wide:
        scratch += [
            pltpu.VMEM((tiles, rows, width), jnp.float32),
            pltpu.VMEM((tiles, rows, width), jnp.bfloat16),
            pltpu.SemaphoreType.DMA((tiles // OUT_GROUP,)),
        ]
    return pl.pallas_call(
        kernel,
        in_specs=[smem] * len(scalars) + [hbm, hbm] + [vmem] * len(tables),
        out_specs=hbm if wide else vmem,
        out_shape=out_shape,
        scratch_shapes=scratch,
        compiler_params=pltpu.CompilerParams(vmem_limit_bytes=58 * 1024 * 1024),
        name=name,
    )(*scalars, nk, queries, *tables)


def pair_lists(code, key_dest, query_tiles):
    devices = code.shape[0]
    most = key_dest.shape[0] * query_tiles
    owned = key_dest[:, None] == jnp.arange(devices, dtype=jnp.int32)[None, :]
    allowed = (code[:, :, 0] > -2).astype(jnp.int32)
    match = jnp.sum(jnp.where(owned[:, :, None], allowed[None], 0), axis=1).reshape(most)
    index = jnp.arange(most, dtype=jnp.int32)
    place = jnp.sum(jnp.where(index[None, :] < index[:, None], match[None, :], 0), axis=1)
    tile = index // query_tiles
    slot = index % query_tiles
    owner = jnp.repeat(key_dest, query_tiles)
    chosen = (place[None, :] == index[:, None]) & (match[None, :] > 0)
    listed = lambda x: jnp.sum(jnp.where(chosen, x[None, :], 0), axis=1)
    pairs = jnp.sum(match)
    spare = index >= pairs
    pair_tile = listed(tile)
    pair_query = jnp.where(spare, owner[0] * query_tiles, listed(owner * query_tiles + slot))
    pair_out = jnp.where(
        spare, owner[0] * 2 * query_tiles, listed(owner * 2 * query_tiles + slot)
    )
    return pair_tile, pair_query, pair_out, pairs.reshape(1)


def shards(key_feats, query_feats, key_dest, key_scene, key_count, pos_tile, pos_row):
    tiles, rows, width = key_feats.shape
    query_tiles = query_feats.shape[0]
    devices = lax.axis_size("cam") * lax.axis_size("lidar")
    queries = lax.all_gather(unit_rows(query_feats), AXES, axis=0, tiled=True)

    device_iota = jnp.arange(devices, dtype=jnp.int32)
    owned = key_dest[None, :] == device_iota[:, None]
    scene_out = jnp.sum(jnp.where(owned, key_scene[None, :] + 1, 0), axis=1)
    scene_in = exchange(scene_out.reshape(devices, 1, 1)).reshape(devices)
    pos_source = pos_tile // tiles
    hit = pos_source[None, :] == device_iota[:, None]
    query_scene = jnp.sum(jnp.where(hit, scene_in[:, None], 0), axis=0)
    same = scene_in[:, None] == query_scene[None, :]
    code = jnp.where(
        hit[:, :, None], pos_row[None, :, :], jnp.where(same[:, :, None], -1, -2)
    )
    code = exchange(code)

    nk = unit_rows(key_feats)
    pair_tile, pair_query, pair_out, pairs = pair_lists(code, key_dest, query_tiles)
    code = code.reshape(devices * query_tiles, rows)
    partial = tile_call(
        functools.partial(total_kernel, query_tiles),
        [pair_tile, pair_query, pair_out, pairs, key_count],
        nk,
        queries,
        [code],
        jax.ShapeDtypeStruct((devices * 2 * query_tiles, rows), jnp.float32),
        4 * TOTAL_GROUP,
        False,
        "totals",
    )
    partial = partial.reshape(devices, 2 * query_tiles, rows)
    arrived = jnp.sum(exchange(partial), axis=0)
    total, picked = arrived[:query_tiles], arrived[query_tiles:]
    scale = exchange(jnp.broadcast_to((1.0 / total)[None], (devices, query_tiles, rows)))
    loss = jnp.log(total) - picked
    key_grad = tile_call(
        grad_kernel,
        [pair_tile, pair_query, pairs, key_count],
        nk,
        queries,
        [code, scale.reshape(devices * query_tiles, rows)],
        jax.ShapeDtypeStruct((tiles, rows, width), jnp.bfloat16),
        3 * GRAD_GROUP,
        True,
        "grads",
    )
    return (loss, key_grad)


def solution(mesh):
    return jax.shard_map(
        shards,
        mesh=mesh,
        in_specs=(
            P(AXES, None, None),
            P(AXES, None, None),
            P(AXES),
            P(AXES),
            P(AXES),
            P(AXES),
            P(AXES, None),
        ),
        out_specs=(P(AXES, None), P(AXES, None, None)),
        check_vma=False,
    )
```

```python
import functools
import math

import jax
import jax.numpy as jnp
from jax import lax
from jax.experimental import pallas as pl
from jax.experimental.pallas import tpu as pltpu
from jax.sharding import PartitionSpec as P

inv_temp = 1.0 / 0.07
log2_scale = inv_temp * math.log2(math.e)
eps = 1e-06
TOTAL_GROUP = 8
EXPO_GROUP = 8
GRAD_GROUP = 8
OUT_GROUP = 8
AXES = ("cam", "lidar")


def unit_rows(x):
    xf = x.astype(jnp.float32)
    scaled = (
        xf * lax.rsqrt(jnp.mean(xf * xf, axis=-1, keepdims=True) + eps) / math.sqrt(x.shape[-1])
    )
    return scaled.astype(jnp.bfloat16)


def exchange(x):
    return lax.all_to_all(x, AXES, split_axis=0, concat_axis=0, tiled=True)


def products(keys, queries):
    return lax.dot_general(
        keys, queries, (((1,), (1,)), ((), ())), preferred_element_type=jnp.float32
    )


def over_pairs(pairs, group, sources, first, body, last=None):
    slots = sources[0][2].shape[0]
    ahead = slots // group - 1
    groups = (pairs + (group - 1)) // group

    def fetch(step, act):
        base = lax.rem(step, ahead + 1) * group
        for j in range(group):
            p = step * group + j
            for hbm, index, buf, sem in sources:
                block = hbm.at[p if index is None else index[p]]
                act(pltpu.make_async_copy(block, buf.at[base + j], sem.at[base + j]))

    start = lambda copy: copy.start()
    for early in range(ahead):

        @pl.when(early < groups)
        def _():
            fetch(early, start)

    first()

    @pl.loop(0, groups)
    def _(step):
        @pl.when(step + ahead < groups)
        def _():
            fetch(step + ahead, start)

        fetch(step, lambda copy: copy.wait())
        base = lax.rem(step, ahead + 1) * group
        for j in range(group):
            body(step * group + j, base + j)
        if last is not None:
            last(step)

    return groups


def total_kernel(
    slots, pair_tile, pair_query, pair_out, pairs, count, nk_hbm, q_hbm, code_ref, out_ref,
    nk_buf, q_buf, nk_sem, q_sem,
):
    row = lax.broadcasted_iota(jnp.int32, (nk_buf.shape[1], code_ref.shape[1]), 0)

    def first():
        out_ref[...] = jnp.zeros_like(out_ref)

    def body(p, slot):
        raw = products(nk_buf[slot], q_buf[slot])
        code = code_ref[pl.ds(pair_query[p], 1), :]
        expo = jnp.where(row < count[pair_tile[p]], jnp.exp2(raw * log2_scale), 0.0)
        total = jnp.sum(expo, axis=0, keepdims=True)
        picked = jnp.sum(jnp.where(row == code, raw, 0.0), axis=0, keepdims=True)
        out_ref[pl.ds(pair_out[p], 1), :] = jnp.where(code > -2, total, 0.0)
        out_ref[pl.ds(pair_out[p] + slots, 1), :] = picked * inv_temp

    sources = [(nk_hbm, pair_tile, nk_buf, nk_sem), (q_hbm, pair_query, q_buf, q_sem)]
    over_pairs(pairs[0], TOTAL_GROUP, sources, first, body)


def expo_kernel(
    pair_tile, pair_query, pairs, count, nk_hbm, q_hbm, out_hbm,
    nk_buf, q_buf, nk_sem, q_sem, out_buf, out_sem,
):
    row = lax.broadcasted_iota(jnp.int32, out_buf.shape[1:], 0)

    def part(step):
        span = pl.ds(step * EXPO_GROUP, EXPO_GROUP)
        return pltpu.make_async_copy(out_buf.at[span], out_hbm.at[span], out_sem.at[step])

    def body(p, slot):
        raw = products(nk_buf[slot], q_buf[slot])
        live = row < count[pair_tile[p]]
        out_buf[p] = jnp.where(live, jnp.exp2(raw * log2_scale), 0.0)

    sources = [(nk_hbm, pair_tile, nk_buf, nk_sem), (q_hbm, pair_query, q_buf, q_sem)]
    send = lambda step: part(step).start()
    groups = over_pairs(pairs[0], EXPO_GROUP, sources, lambda: None, body, send)

    @pl.loop(0, groups)
    def _(step):
        part(step).wait()


def grad_kernel(
    pair_tile, pair_query, pairs, expo_hbm, q_hbm, code_ref, scale_ref, out_hbm,
    expo_buf, q_buf, expo_sem, q_sem, sum_buf, out_buf, out_sem,
):
    row = lax.broadcasted_iota(jnp.int32, expo_buf.shape[1:], 0)

    def first():
        sum_buf[...] = jnp.zeros_like(sum_buf)

    def body(p, slot):
        tile, query = pair_tile[p], pair_query[p]
        code = jnp.where(p < pairs[0], code_ref[pl.ds(query, 1), :], -2)
        scale = jnp.where(code > -2, scale_ref[pl.ds(query, 1), :], 0.0)
        target = jnp.where(row == code, 1.0, 0.0)
        weights = (expo_buf[slot] * scale - target).astype(jnp.bfloat16)
        sum_buf[tile] += jnp.dot(weights, q_buf[slot], preferred_element_type=jnp.float32)

    sources = [(expo_hbm, None, expo_buf, expo_sem), (q_hbm, pair_query, q_buf, q_sem)]
    over_pairs(pairs[0], GRAD_GROUP, sources, first, body)

    def part(group):
        span = pl.ds(group * OUT_GROUP, OUT_GROUP)
        return pltpu.make_async_copy(out_buf.at[span], out_hbm.at[span], out_sem.at[group])

    groups = out_sem.shape[0]

    @pl.loop(0, groups)
    def _(group):
        for j in range(OUT_GROUP):
            tile = group * OUT_GROUP + j
            out_buf[tile] = (sum_buf[tile] * inv_temp).astype(jnp.bfloat16)
        part(group).start()

    @pl.loop(0, groups)
    def _(group):
        part(group).wait()


def tile_call(kernel, scalars, blocks, tables, out_shape, slots, wide, name):
    smem, vmem, hbm = (pl.BlockSpec(memory_space=m) for m in (pltpu.SMEM, pltpu.VMEM, pl.ANY))
    most = scalars[0].shape[0]
    rows, width = blocks[1].shape[1:]
    scratch = [pltpu.VMEM((slots,) + block.shape[1:], block.dtype) for block in blocks]
    scratch += [pltpu.SemaphoreType.DMA((slots,)) for block in blocks]
    return pl.pallas_call(
        kernel,
        in_specs=[smem] * len(scalars) + [hbm] * len(blocks) + [vmem] * len(tables),
        out_specs=hbm if wide else vmem,
        out_shape=out_shape,
        scratch_shapes=scratch + wide,
        cost_estimate=pl.CostEstimate(
            flops=2 * most * rows * rows * width,
            bytes_accessed=4 * most * rows * width,
            transcendentals=most * rows * rows,
        ),
        compiler_params=pltpu.CompilerParams(vmem_limit_bytes=58 * 1024 * 1024),
        name=name,
    )(*scalars, *blocks, *tables)


def pair_lists(code, key_dest, query_tiles):
    devices = code.shape[0]
    most = key_dest.shape[0] * query_tiles
    owned = key_dest[:, None] == jnp.arange(devices, dtype=jnp.int32)[None, :]
    allowed = (code[:, :, 0] > -2).astype(jnp.int32)
    match = jnp.sum(jnp.where(owned[:, :, None], allowed[None], 0), axis=1).reshape(most)
    index = jnp.arange(most, dtype=jnp.int32)
    place = jnp.sum(jnp.where(index[None, :] < index[:, None], match[None, :], 0), axis=1)
    tile = index // query_tiles
    slot = index % query_tiles
    owner = jnp.repeat(key_dest, query_tiles)
    chosen = (place[None, :] == index[:, None]) & (match[None, :] > 0)
    listed = lambda x: jnp.sum(jnp.where(chosen, x[None, :], 0), axis=1)
    pairs = jnp.sum(match)
    spare = index >= pairs
    pair_tile = listed(tile)
    pair_query = jnp.where(spare, owner[0] * query_tiles, listed(owner * query_tiles + slot))
    pair_out = jnp.where(
        spare, owner[0] * 2 * query_tiles, listed(owner * 2 * query_tiles + slot)
    )
    return pair_tile, pair_query, pair_out, pairs.reshape(1)


def shards(key_feats, query_feats, key_dest, key_scene, key_count, pos_tile, pos_row):
    tiles, rows, width = key_feats.shape
    query_tiles = query_feats.shape[0]
    devices = lax.axis_size("cam") * lax.axis_size("lidar")
    queries = lax.all_gather(unit_rows(query_feats), AXES, axis=0, tiled=True)

    device_iota = jnp.arange(devices, dtype=jnp.int32)
    owned = key_dest[None, :] == device_iota[:, None]
    scene_out = jnp.sum(jnp.where(owned, key_scene[None, :] + 1, 0), axis=1)
    scene_in = exchange(scene_out.reshape(devices, 1, 1)).reshape(devices)
    pos_source = pos_tile // tiles
    hit = pos_source[None, :] == device_iota[:, None]
    query_scene = jnp.sum(jnp.where(hit, scene_in[:, None], 0), axis=0)
    same = scene_in[:, None] == query_scene[None, :]
    code = jnp.where(
        hit[:, :, None], pos_row[None, :, :], jnp.where(same[:, :, None], -1, -2)
    )
    code = exchange(code)

    nk = unit_rows(key_feats)
    pair_tile, pair_query, pair_out, pairs = pair_lists(code, key_dest, query_tiles)
    code = code.reshape(devices * query_tiles, rows)
    partial = tile_call(
        functools.partial(total_kernel, query_tiles),
        [pair_tile, pair_query, pair_out, pairs, key_count],
        [nk, queries],
        [code],
        jax.ShapeDtypeStruct((devices * 2 * query_tiles, rows), jnp.float32),
        4 * TOTAL_GROUP,
        [],
        "totals",
    )
    partial, pairs = lax.optimization_barrier((partial, pairs))
    most = pair_tile.shape[0]
    expo_shape = jax.ShapeDtypeStruct((most, rows, rows), jnp.float32)
    expo = tile_call(
        expo_kernel,
        [pair_tile, pair_query, pairs, key_count],
        [nk, queries],
        [],
        expo_shape,
        4 * EXPO_GROUP,
        [
            pltpu.VMEM(expo_shape.shape, jnp.float32),
            pltpu.SemaphoreType.DMA((most // EXPO_GROUP,)),
        ],
        "expos",
    )
    partial = partial.reshape(devices, 2 * query_tiles, rows)
    arrived, expo = lax.optimization_barrier((exchange(partial), expo))
    arrived = jnp.sum(arrived, axis=0)
    total, picked = arrived[:query_tiles], arrived[query_tiles:]
    scale = exchange(jnp.broadcast_to((1.0 / total)[None], (devices, query_tiles, rows)))
    loss = jnp.log(total) - picked
    key_grad = tile_call(
        grad_kernel,
        [pair_tile, pair_query, pairs],
        [expo, queries],
        [code, scale.reshape(devices * query_tiles, rows)],
        jax.ShapeDtypeStruct((tiles, rows, width), jnp.bfloat16),
        5 * GRAD_GROUP,
        [
            pltpu.VMEM((tiles, rows, width), jnp.float32),
            pltpu.VMEM((tiles, rows, width), jnp.bfloat16),
            pltpu.SemaphoreType.DMA((tiles // OUT_GROUP,)),
        ],
        "grads",
    )
    return (loss, key_grad)


def solution(mesh):
    return jax.shard_map(
        shards,
        mesh=mesh,
        in_specs=(
            P(AXES, None, None),
            P(AXES, None, None),
            P(AXES),
            P(AXES),
            P(AXES),
            P(AXES),
            P(AXES, None),
        ),
        out_specs=(P(AXES, None), P(AXES, None, None)),
        check_vma=False,
    )
```

```python
import functools
import math

import jax
import jax.numpy as jnp
from jax import lax
from jax.experimental import pallas as pl
from jax.experimental.pallas import tpu as pltpu
from jax.sharding import PartitionSpec as P

inv_temp = 1.0 / 0.07
log2_scale = inv_temp * math.log2(math.e)
eps = 1e-06
TOTAL_GROUP = 8
GRAD_GROUP = 8
OUT_GROUP = 8
AXES = ("cam", "lidar")


def unit_rows(x):
    xf = x.astype(jnp.float32)
    scaled = (
        xf * lax.rsqrt(jnp.mean(xf * xf, axis=-1, keepdims=True) + eps) / math.sqrt(x.shape[-1])
    )
    return scaled.astype(jnp.bfloat16)


def exchange(x):
    return lax.all_to_all(x, AXES, split_axis=0, concat_axis=0, tiled=True)


def products(keys, queries):
    return lax.dot_general(
        keys, queries, (((1,), (1,)), ((), ())), preferred_element_type=jnp.float32
    )


def over_pairs(pairs, group, sources, first, body, last=None):
    slots = sources[0][2].shape[0]
    ahead = slots // group - 1
    groups = (pairs + (group - 1)) // group

    def fetch(step, act):
        base = lax.rem(step, ahead + 1) * group
        for j in range(group):
            p = step * group + j
            for hbm, index, buf, sem in sources:
                block = hbm.at[p if index is None else index[p]]
                act(pltpu.make_async_copy(block, buf.at[base + j], sem.at[base + j]))

    start = lambda copy: copy.start()
    for early in range(ahead):

        @pl.when(early < groups)
        def _():
            fetch(early, start)

    first()

    @pl.loop(0, groups)
    def _(step):
        @pl.when(step + ahead < groups)
        def _():
            fetch(step + ahead, start)

        fetch(step, lambda copy: copy.wait())
        base = lax.rem(step, ahead + 1) * group
        for j in range(group):
            body(step * group + j, base + j)
        if last is not None:
            last(step)

    return groups


def total_kernel(
    slots, pair_tile, pair_query, pair_out, pairs, count, nk_hbm, q_hbm, code_ref,
    out_ref, expo_hbm, nk_buf, q_buf, nk_sem, q_sem, expo_buf, expo_sem,
):
    def part(step):
        span = pl.ds(step * TOTAL_GROUP, TOTAL_GROUP)
        return pltpu.make_async_copy(expo_buf.at[span], expo_hbm.at[span], expo_sem.at[step])

    row = lax.broadcasted_iota(jnp.int32, (nk_buf.shape[1], code_ref.shape[1]), 0)

    def first():
        out_ref[...] = jnp.zeros_like(out_ref)

    def body(p, slot):
        raw = products(nk_buf[slot], q_buf[slot])
        code = code_ref[pl.ds(pair_query[p], 1), :]
        expo = jnp.where(row < count[pair_tile[p]], jnp.exp2(raw * log2_scale), 0.0)
        expo_buf[p] = expo
        total = jnp.sum(expo, axis=0, keepdims=True)
        picked = jnp.sum(jnp.where(row == code, raw, 0.0), axis=0, keepdims=True)
        out_ref[pl.ds(pair_out[p], 1), :] = jnp.where(code > -2, total, 0.0)
        out_ref[pl.ds(pair_out[p] + slots, 1), :] = picked * inv_temp

    sources = [(nk_hbm, pair_tile, nk_buf, nk_sem), (q_hbm, pair_query, q_buf, q_sem)]
    send = lambda step: part(step).start()
    groups = over_pairs(pairs[0], TOTAL_GROUP, sources, first, body, send)

    @pl.loop(0, groups)
    def _(step):
        part(step).wait()


def grad_kernel(
    pair_tile, pair_query, pairs, expo_hbm, q_hbm, code_ref, scale_ref, out_hbm,
    expo_buf, q_buf, expo_sem, q_sem, sum_buf, out_buf, out_sem, sent,
):
    row = lax.broadcasted_iota(jnp.int32, expo_buf.shape[1:], 0)
    most = pair_tile.shape[0]
    tiles = out_hbm.shape[0]

    def part(group):
        span = pl.ds(group * OUT_GROUP, OUT_GROUP)
        return pltpu.make_async_copy(out_buf.at[span], out_hbm.at[span], out_sem.at[group])

    def send_until(tile):
        ready = jnp.maximum(tile // OUT_GROUP, sent[0])

        @pl.loop(sent[0], ready)
        def _(group):
            part(group).start()

        sent[0] = ready

    def first():
        out_buf[...] = jnp.zeros_like(out_buf)
        sum_buf[...] = jnp.zeros_like(sum_buf)
        sent[0] = 0

    def body(p, slot):
        valid = p < pairs[0]
        tile, query = pair_tile[p], pair_query[p]
        code = code_ref[pl.ds(query, 1), :]
        scale = jnp.where(code > -2, scale_ref[pl.ds(query, 1), :], 0.0)
        target = jnp.where(row == code, 1.0, 0.0)
        weights = (expo_buf[slot] * scale - target).astype(jnp.bfloat16)
        grad = jnp.dot(weights, q_buf[slot], preferred_element_type=jnp.float32)
        same = pair_tile[jnp.maximum(p - 1, 0)] == tile
        grad = jnp.where(same, sum_buf[...], 0.0) + grad
        sum_buf[...] = grad
        out_buf[jnp.where(valid, tile, tiles)] = (grad * inv_temp).astype(jnp.bfloat16)

    def last(step):
        ahead = (step + 1) * GRAD_GROUP
        send_until(jnp.where(ahead < pairs[0], pair_tile[jnp.minimum(ahead, most - 1)], 0))

    sources = [(expo_hbm, None, expo_buf, expo_sem), (q_hbm, pair_query, q_buf, q_sem)]
    over_pairs(pairs[0], GRAD_GROUP, sources, first, body, last)
    send_until(tiles)

    @pl.loop(0, tiles // OUT_GROUP)
    def _(group):
        part(group).wait()


def tile_call(kernel, scalars, blocks, tables, out_shape, out_spaces, slots, wide, name):
    smem, vmem, hbm = (pl.BlockSpec(memory_space=m) for m in (pltpu.SMEM, pltpu.VMEM, pl.ANY))
    most = scalars[0].shape[0]
    rows, width = blocks[1].shape[1:]
    scratch = [pltpu.VMEM((slots,) + block.shape[1:], block.dtype) for block in blocks]
    scratch += [pltpu.SemaphoreType.DMA((slots,)) for block in blocks]
    return pl.pallas_call(
        kernel,
        in_specs=[smem] * len(scalars) + [hbm] * len(blocks) + [vmem] * len(tables),
        out_specs=[pl.BlockSpec(memory_space=m) for m in out_spaces],
        out_shape=out_shape,
        scratch_shapes=scratch + wide,
        cost_estimate=pl.CostEstimate(
            flops=2 * most * rows * rows * width,
            bytes_accessed=4 * most * rows * width,
            transcendentals=most * rows * rows,
        ),
        compiler_params=pltpu.CompilerParams(vmem_limit_bytes=58 * 1024 * 1024),
        name=name,
    )(*scalars, *blocks, *tables)


def pair_lists(code, key_dest, query_tiles):
    devices = code.shape[0]
    most = key_dest.shape[0] * query_tiles
    owned = key_dest[:, None] == jnp.arange(devices, dtype=jnp.int32)[None, :]
    allowed = (code[:, :, 0] > -2).astype(jnp.int32)
    match = jnp.sum(jnp.where(owned[:, :, None], allowed[None], 0), axis=1).reshape(most)
    index = jnp.arange(most, dtype=jnp.int32)
    place = jnp.sum(jnp.where(index[None, :] < index[:, None], match[None, :], 0), axis=1)
    tile = index // query_tiles
    slot = index % query_tiles
    owner = jnp.repeat(key_dest, query_tiles)
    chosen = (place[None, :] == index[:, None]) & (match[None, :] > 0)
    listed = lambda x: jnp.sum(jnp.where(chosen, x[None, :], 0), axis=1)
    pairs = jnp.sum(match)
    spare = index >= pairs
    pair_tile = listed(tile)
    pair_query = jnp.where(spare, owner[0] * query_tiles, listed(owner * query_tiles + slot))
    pair_out = jnp.where(
        spare, owner[0] * 2 * query_tiles, listed(owner * 2 * query_tiles + slot)
    )
    return pair_tile, pair_query, pair_out, pairs.reshape(1)


def shards(key_feats, query_feats, key_dest, key_scene, key_count, pos_tile, pos_row):
    tiles, rows, width = key_feats.shape
    query_tiles = query_feats.shape[0]
    devices = lax.axis_size("cam") * lax.axis_size("lidar")
    queries = lax.all_gather(unit_rows(query_feats), AXES, axis=0, tiled=True)

    device_iota = jnp.arange(devices, dtype=jnp.int32)
    owned = key_dest[None, :] == device_iota[:, None]
    scene_out = jnp.sum(jnp.where(owned, key_scene[None, :] + 1, 0), axis=1)
    scene_in = exchange(scene_out.reshape(devices, 1, 1)).reshape(devices)
    pos_source = pos_tile // tiles
    hit = pos_source[None, :] == device_iota[:, None]
    query_scene = jnp.sum(jnp.where(hit, scene_in[:, None], 0), axis=0)
    same = scene_in[:, None] == query_scene[None, :]
    code = jnp.where(
        hit[:, :, None], pos_row[None, :, :], jnp.where(same[:, :, None], -1, -2)
    )
    code = exchange(code)

    nk = unit_rows(key_feats)
    pair_tile, pair_query, pair_out, pairs = pair_lists(code, key_dest, query_tiles)
    code = code.reshape(devices * query_tiles, rows)
    most = pair_tile.shape[0]
    expo_shape = jax.ShapeDtypeStruct((most, rows, rows), jnp.float32)
    partial, expo = tile_call(
        functools.partial(total_kernel, query_tiles),
        [pair_tile, pair_query, pair_out, pairs, key_count],
        [nk, queries],
        [code],
        [jax.ShapeDtypeStruct((devices * 2 * query_tiles, rows), jnp.float32), expo_shape],
        [pltpu.VMEM, pl.ANY],
        4 * TOTAL_GROUP,
        [
            pltpu.VMEM(expo_shape.shape, jnp.float32),
            pltpu.SemaphoreType.DMA((most // TOTAL_GROUP,)),
        ],
        "totals",
    )
    partial = partial.reshape(devices, 2 * query_tiles, rows)
    arrived = jnp.sum(exchange(partial), axis=0)
    total, picked = arrived[:query_tiles], arrived[query_tiles:]
    scale = exchange(jnp.broadcast_to((1.0 / total)[None], (devices, query_tiles, rows)))
    loss = jnp.log(total) - picked
    (key_grad,) = tile_call(
        grad_kernel,
        [pair_tile, pair_query, pairs],
        [expo, queries],
        [code, scale.reshape(devices * query_tiles, rows)],
        [jax.ShapeDtypeStruct((tiles, rows, width), jnp.bfloat16)],
        [pl.ANY],
        5 * GRAD_GROUP,
        [
            pltpu.VMEM((rows, width), jnp.float32),
            pltpu.VMEM((tiles + 1, rows, width), jnp.bfloat16),
            pltpu.SemaphoreType.DMA((tiles // OUT_GROUP,)),
            pltpu.SMEM((1,), jnp.int32),
        ],
        "grads",
    )
    return (loss, key_grad)


def solution(mesh):
    return jax.shard_map(
        shards,
        mesh=mesh,
        in_specs=(
            P(AXES, None, None),
            P(AXES, None, None),
            P(AXES),
            P(AXES),
            P(AXES),
            P(AXES),
            P(AXES, None),
        ),
        out_specs=(P(AXES, None), P(AXES, None, None)),
        check_vma=False,
    )
```

```python
import functools
import math

import jax
import jax.numpy as jnp
from jax import lax
from jax.experimental import pallas as pl
from jax.experimental.pallas import tpu as pltpu
from jax.sharding import PartitionSpec as P

inv_temp = 1.0 / 0.07
log2_scale = inv_temp * math.log2(math.e)
eps = 1e-06
TOTAL_GROUP = 8
TOTAL_AHEAD = 3
GRAD_GROUP = 8
OUT_GROUP = 8
TOTAL_MIB = 5
GRAD_MIB = 5
SHARE_MIB = 2
AXES = ("cam", "lidar")


def unit_rows(x):
    xf = x.astype(jnp.float32)
    scaled = (
        xf * lax.rsqrt(jnp.mean(xf * xf, axis=-1, keepdims=True) + eps) / math.sqrt(x.shape[-1])
    )
    return scaled.astype(jnp.bfloat16)


def exchange(x):
    return lax.all_to_all(x, AXES, split_axis=0, concat_axis=0, tiled=True)


def products(keys, queries):
    return lax.dot_general(
        keys, queries, (((1,), (1,)), ((), ())), preferred_element_type=jnp.float32
    )


def over_pairs(pairs, group, ahead, sources, first, body, last=None):
    groups = (pairs + (group - 1)) // group

    def fetch(step, act):
        base = lax.rem(step, ahead + 1) * group
        for j in range(group):
            p = step * group + j
            for hbm, index, buf, sem, ring in sources:
                place = buf.at[base + j if ring else p]
                act(pltpu.make_async_copy(hbm.at[index[p]], place, sem.at[base + j]))

    start = lambda copy: copy.start()
    for early in range(ahead):

        @pl.when(early < groups)
        def _():
            fetch(early, start)

    first()

    @pl.loop(0, groups)
    def _(step):
        @pl.when(step + ahead < groups)
        def _():
            fetch(step + ahead, start)

        fetch(step, lambda copy: copy.wait())
        base = lax.rem(step, ahead + 1) * group
        for j in range(group):
            body(step * group + j, base + j)
        if last is not None:
            last(step)


def total_kernel(
    half, pair_tile, pair_query, pair_out, pairs, count, nk_hbm, q_hbm, code_ref,
    out_ref, expo_ref, q_ref, nk_buf, nk_sem, q_sem,
):
    row = lax.broadcasted_iota(jnp.int32, expo_ref.shape[1:], 0)

    def first():
        out_ref[...] = jnp.zeros_like(out_ref)

    def body(p, slot):
        raw = products(nk_buf[slot], q_ref[p])
        code = code_ref[pl.ds(pair_query[p], 1), :]
        expo = jnp.where(row < count[pair_tile[p]], jnp.exp2(raw * log2_scale), 0.0)
        expo_ref[p] = expo
        total = jnp.sum(expo, axis=0, keepdims=True)
        picked = jnp.sum(jnp.where(row == code, raw, 0.0), axis=0, keepdims=True)
        out_ref[pl.ds(pair_out[p], 1), :] = jnp.where(code > -2, total, 0.0)
        out_ref[pl.ds(pair_out[p] + half, 1), :] = picked * inv_temp

    sources = [
        (nk_hbm, pair_tile, nk_buf, nk_sem, True),
        (q_hbm, pair_query, q_ref, q_sem, False),
    ]
    over_pairs(pairs[0], TOTAL_GROUP, TOTAL_AHEAD, sources, first, body)


def share_kernel(arrived_ref, scale_ref, loss_ref):
    half = loss_ref.shape[0]
    sums = jnp.sum(arrived_ref[...], axis=0)
    total = sums[:half]
    loss_ref[...] = jnp.log(total) - sums[half:]
    scale_ref[...] = jnp.broadcast_to((1.0 / total)[None], scale_ref.shape)


def grad_kernel(
    pair_tile, pair_query, pairs, expo_ref, q_ref, code_ref, scale_ref, out_hbm,
    sum_buf, out_buf, out_sem, sent,
):
    row = lax.broadcasted_iota(jnp.int32, expo_ref.shape[1:], 0)
    most = pair_tile.shape[0]
    tiles = out_hbm.shape[0]

    def part(group):
        span = pl.ds(group * OUT_GROUP, OUT_GROUP)
        return pltpu.make_async_copy(out_buf.at[span], out_hbm.at[span], out_sem.at[group])

    def send_until(tile):
        ready = jnp.maximum(tile // OUT_GROUP, sent[0])

        @pl.loop(sent[0], ready)
        def _(group):
            part(group).start()

        sent[0] = ready

    def first():
        out_buf[...] = jnp.zeros_like(out_buf)
        sum_buf[...] = jnp.zeros_like(sum_buf)
        sent[0] = 0

    def body(p, slot):
        valid = p < pairs[0]
        tile, query = pair_tile[p], pair_query[p]
        code = code_ref[pl.ds(query, 1), :]
        scale = jnp.where(code > -2, scale_ref[pl.ds(query, 1), :], 0.0)
        target = jnp.where(row == code, 1.0, 0.0)
        weights = (expo_ref[p] * scale - target).astype(jnp.bfloat16)
        grad = jnp.dot(weights, q_ref[p], preferred_element_type=jnp.float32)
        same = pair_tile[jnp.maximum(p - 1, 0)] == tile
        grad = jnp.where(same, sum_buf[...], 0.0) + grad
        sum_buf[...] = grad
        out_buf[jnp.where(valid, tile, tiles)] = (grad * inv_temp).astype(jnp.bfloat16)

    def last(step):
        ahead = (step + 1) * GRAD_GROUP
        send_until(jnp.where(ahead < pairs[0], pair_tile[jnp.minimum(ahead, most - 1)], 0))

    over_pairs(pairs[0], GRAD_GROUP, 0, [], first, body, last)
    send_until(tiles)

    @pl.loop(0, tiles // OUT_GROUP)
    def _(group):
        part(group).wait()


def tile_call(kernel, operands, out_shape, out_spaces, scratch, vmem_mib, name):
    return pl.pallas_call(
        kernel,
        in_specs=[pl.BlockSpec(memory_space=space) for space, _ in operands],
        out_specs=[pl.BlockSpec(memory_space=space) for space in out_spaces],
        out_shape=out_shape,
        scratch_shapes=scratch,
        compiler_params=pltpu.CompilerParams(vmem_limit_bytes=vmem_mib * 1024 * 1024),
        name=name,
    )(*[x for _, x in operands])


def in_space(space, arrays):
    return [(space, x) for x in arrays]


def pair_lists(code, key_dest, query_tiles):
    devices = code.shape[0]
    most = key_dest.shape[0] * query_tiles
    owned = key_dest[:, None] == jnp.arange(devices, dtype=jnp.int32)[None, :]
    allowed = (code[:, :, 0] > -2).astype(jnp.int32)
    match = jnp.sum(jnp.where(owned[:, :, None], allowed[None], 0), axis=1).reshape(most)
    index = jnp.arange(most, dtype=jnp.int32)
    place = jnp.sum(jnp.where(index[None, :] < index[:, None], match[None, :], 0), axis=1)
    tile = index // query_tiles
    slot = index % query_tiles
    owner = jnp.repeat(key_dest, query_tiles)
    chosen = (place[None, :] == index[:, None]) & (match[None, :] > 0)
    listed = lambda x: jnp.sum(jnp.where(chosen, x[None, :], 0), axis=1)
    pairs = jnp.sum(match)
    spare = index >= pairs
    pair_tile = listed(tile)
    pair_query = jnp.where(spare, owner[0] * query_tiles, listed(owner * query_tiles + slot))
    pair_out = jnp.where(
        spare, owner[0] * 2 * query_tiles, listed(owner * 2 * query_tiles + slot)
    )
    return pair_tile, pair_query, pair_out, pairs.reshape(1)


def shards(key_feats, query_feats, key_dest, key_scene, key_count, pos_tile, pos_row):
    tiles, rows, width = key_feats.shape
    query_tiles = query_feats.shape[0]
    devices = lax.axis_size("cam") * lax.axis_size("lidar")
    queries = lax.all_gather(unit_rows(query_feats), AXES, axis=0, tiled=True)

    device_iota = jnp.arange(devices, dtype=jnp.int32)
    owned = key_dest[None, :] == device_iota[:, None]
    scene_out = jnp.sum(jnp.where(owned, key_scene[None, :] + 1, 0), axis=1)
    scene_in = exchange(scene_out.reshape(devices, 1, 1)).reshape(devices)
    pos_source = pos_tile // tiles
    hit = pos_source[None, :] == device_iota[:, None]
    query_scene = jnp.sum(jnp.where(hit, scene_in[:, None], 0), axis=0)
    same = scene_in[:, None] == query_scene[None, :]
    code = jnp.where(
        hit[:, :, None], pos_row[None, :, :], jnp.where(same[:, :, None], -1, -2)
    )
    code = exchange(code)

    nk = unit_rows(key_feats)
    pair_tile, pair_query, pair_out, pairs = pair_lists(code, key_dest, query_tiles)
    code = code.reshape(devices * query_tiles, rows)
    most = pair_tile.shape[0]
    slots = (TOTAL_AHEAD + 1) * TOTAL_GROUP
    partial, expo, picks = tile_call(
        functools.partial(total_kernel, query_tiles),
        in_space(pltpu.SMEM, [pair_tile, pair_query, pair_out, pairs, key_count])
        + in_space(pl.ANY, [nk, queries])
        + in_space(pltpu.VMEM, [code]),
        [
            jax.ShapeDtypeStruct((devices * 2 * query_tiles, rows), jnp.float32),
            pltpu.VMEM((most, rows, rows), jnp.float32),
            pltpu.VMEM((most, rows, width), jnp.bfloat16),
        ],
        [pltpu.VMEM] * 3,
        [
            pltpu.VMEM((slots, rows, width), jnp.bfloat16),
            pltpu.SemaphoreType.DMA((slots,)),
            pltpu.SemaphoreType.DMA((slots,)),
        ],
        TOTAL_MIB,
        "totals",
    )
    expo = pltpu.with_memory_space_constraint(expo, pltpu.VMEM)
    picks = pltpu.with_memory_space_constraint(picks, pltpu.VMEM)
    partial = partial.reshape(devices, 2 * query_tiles, rows)
    scale, loss = tile_call(
        share_kernel,
        in_space(pltpu.VMEM, [exchange(partial)]),
        [
            jax.ShapeDtypeStruct((devices, query_tiles, rows), jnp.float32),
            jax.ShapeDtypeStruct((query_tiles, rows), jnp.float32),
        ],
        [pltpu.VMEM] * 2,
        [],
        SHARE_MIB,
        "share",
    )
    scale = exchange(scale)
    (key_grad,) = tile_call(
        grad_kernel,
        in_space(pltpu.SMEM, [pair_tile, pair_query, pairs])
        + in_space(pltpu.VMEM, [expo, picks, code, scale.reshape(devices * query_tiles, rows)]),
        [jax.ShapeDtypeStruct((tiles, rows, width), jnp.bfloat16)],
        [pl.ANY],
        [
            pltpu.VMEM((rows, width), jnp.float32),
            pltpu.VMEM((tiles + 1, rows, width), jnp.bfloat16),
            pltpu.SemaphoreType.DMA((tiles // OUT_GROUP,)),
            pltpu.SMEM((1,), jnp.int32),
        ],
        GRAD_MIB,
        "grads",
    )
    return (loss, key_grad)


def solution(mesh):
    return jax.shard_map(
        shards,
        mesh=mesh,
        in_specs=(
            P(AXES, None, None),
            P(AXES, None, None),
            P(AXES),
            P(AXES),
            P(AXES),
            P(AXES),
            P(AXES, None),
        ),
        out_specs=(P(AXES, None), P(AXES, None, None)),
        check_vma=False,
    )
```

```python
import functools
import math

import jax
import jax.numpy as jnp
from jax import lax
from jax.experimental import pallas as pl
from jax.experimental.pallas import tpu as pltpu
from jax.sharding import PartitionSpec as P

inv_temp = 1.0 / 0.07
log2_scale = inv_temp * math.log2(math.e)
eps = 1e-06
TOTAL_GROUP = 8
TOTAL_AHEAD = 3
GRAD_GROUP = 8
OUT_GROUP = 8
TOTAL_MIB = 5
GRAD_MIB = 5
SHARE_MIB = 2
AXES = ("cam", "lidar")


def unit_rows(x):
    xf = x.astype(jnp.float32)
    scaled = (
        xf * lax.rsqrt(jnp.mean(xf * xf, axis=-1, keepdims=True) + eps) / math.sqrt(x.shape[-1])
    )
    return scaled.astype(jnp.bfloat16)


def exchange(x):
    return lax.all_to_all(x, AXES, split_axis=0, concat_axis=0, tiled=True)


def products(keys, queries):
    return lax.dot_general(
        keys, queries, (((1,), (1,)), ((), ())), preferred_element_type=jnp.float32
    )


def over_pairs(pairs, group, ahead, sources, first, body, last=None):
    groups = (pairs + (group - 1)) // group

    def fetch(step, act):
        base = lax.rem(step, ahead + 1) * group
        for j in range(group):
            p = step * group + j
            for hbm, index, buf, sem, ring in sources:
                place = buf.at[base + j if ring else p]
                act(pltpu.make_async_copy(hbm.at[index[p]], place, sem.at[base + j]))

    start = lambda copy: copy.start()
    for early in range(ahead):

        @pl.when(early < groups)
        def _():
            fetch(early, start)

    first()

    @pl.loop(0, groups)
    def _(step):
        @pl.when(step + ahead < groups)
        def _():
            fetch(step + ahead, start)

        fetch(step, lambda copy: copy.wait())
        base = lax.rem(step, ahead + 1) * group
        for j in range(group):
            body(step * group + j, base + j)
        if last is not None:
            last(step)


def total_kernel(
    half, pair_tile, pair_query, pair_out, pairs, count, nk_hbm, q_hbm, code_ref,
    out_ref, expo_ref, q_ref, nk_buf, nk_sem, q_sem,
):
    row = lax.broadcasted_iota(jnp.int32, expo_ref.shape[1:], 0)

    def first():
        out_ref[...] = jnp.zeros_like(out_ref)

    def body(p, slot):
        raw = products(nk_buf[slot], q_ref[p])
        code = code_ref[pl.ds(pair_query[p], 1), :]
        expo = jnp.where(row < count[pair_tile[p]], jnp.exp2(raw * log2_scale), 0.0)
        expo_ref[p] = expo
        total = jnp.sum(expo, axis=0, keepdims=True)
        picked = jnp.sum(jnp.where(row == code, raw, 0.0), axis=0, keepdims=True)
        out_ref[pl.ds(pair_out[p], 1), :] = jnp.where(code > -2, total, 0.0)
        out_ref[pl.ds(pair_out[p] + half, 1), :] = picked * inv_temp

    sources = [
        (nk_hbm, pair_tile, nk_buf, nk_sem, True),
        (q_hbm, pair_query, q_ref, q_sem, False),
    ]
    over_pairs(pairs[0], TOTAL_GROUP, TOTAL_AHEAD, sources, first, body)


def share_kernel(arrived_ref, scale_ref, loss_ref):
    half = loss_ref.shape[0]
    sums = jnp.sum(arrived_ref[...], axis=0)
    total = sums[:half]
    loss_ref[...] = jnp.log(total) - sums[half:]
    scale_ref[...] = jnp.broadcast_to((1.0 / total)[None], scale_ref.shape)


def grad_kernel(
    pair_tile, pair_query, pairs, expo_ref, q_ref, code_ref, scale_ref, out_hbm,
    sum_buf, out_buf, out_sem, sent,
):
    row = lax.broadcasted_iota(jnp.int32, expo_ref.shape[1:], 0)
    most = pair_tile.shape[0]
    tiles = out_hbm.shape[0]

    def part(group):
        span = pl.ds(group * OUT_GROUP, OUT_GROUP)
        return pltpu.make_async_copy(out_buf.at[span], out_hbm.at[span], out_sem.at[group])

    def send_until(tile):
        ready = jnp.maximum(tile // OUT_GROUP, sent[0])

        @pl.loop(sent[0], ready)
        def _(group):
            part(group).start()

        sent[0] = ready

    def first():
        out_buf[...] = jnp.zeros_like(out_buf)
        sum_buf[...] = jnp.zeros_like(sum_buf)
        sent[0] = 0

    def body(p, slot):
        valid = p < pairs[0]
        tile, query = pair_tile[p], pair_query[p]
        code = code_ref[pl.ds(query, 1), :]
        scale = jnp.where(code > -2, scale_ref[pl.ds(query, 1), :], 0.0)
        target = jnp.where(row == code, 1.0, 0.0)
        weights = (expo_ref[p] * scale - target).astype(jnp.bfloat16)
        grad = jnp.dot(weights, q_ref[p], preferred_element_type=jnp.float32)
        same = pair_tile[jnp.maximum(p - 1, 0)] == tile
        grad = jnp.where(same, sum_buf[...], 0.0) + grad
        sum_buf[...] = grad
        out_buf[jnp.where(valid, tile, tiles)] = (grad * inv_temp).astype(jnp.bfloat16)

    def last(step):
        ahead = (step + 1) * GRAD_GROUP
        send_until(jnp.where(ahead < pairs[0], pair_tile[jnp.minimum(ahead, most - 1)], 0))

    over_pairs(pairs[0], GRAD_GROUP, 0, [], first, body, last)
    send_until(tiles)

    @pl.loop(0, tiles // OUT_GROUP)
    def _(group):
        part(group).wait()


def tile_call(kernel, operands, out_shape, out_spaces, scratch, vmem_mib, name):
    return pl.pallas_call(
        kernel,
        in_specs=[pl.BlockSpec(memory_space=space) for space, _ in operands],
        out_specs=[pl.BlockSpec(memory_space=space) for space in out_spaces],
        out_shape=out_shape,
        scratch_shapes=scratch,
        compiler_params=pltpu.CompilerParams(vmem_limit_bytes=vmem_mib * 1024 * 1024),
        name=name,
    )(*[x for _, x in operands])


def in_space(space, arrays):
    return [(space, x) for x in arrays]


def pair_lists(code, key_dest, query_tiles):
    devices = code.shape[0]
    most = key_dest.shape[0] * query_tiles
    owned = key_dest[:, None] == jnp.arange(devices, dtype=jnp.int32)[None, :]
    allowed = (code[:, :, 0] > -2).astype(jnp.int32)
    match = jnp.sum(jnp.where(owned[:, :, None], allowed[None], 0), axis=1).reshape(most)
    index = jnp.arange(most, dtype=jnp.int32)
    place = jnp.sum(jnp.where(index[None, :] < index[:, None], match[None, :], 0), axis=1)
    tile = index // query_tiles
    slot = index % query_tiles
    owner = jnp.repeat(key_dest, query_tiles)
    chosen = (place[None, :] == index[:, None]) & (match[None, :] > 0)
    listed = lambda x: jnp.sum(jnp.where(chosen, x[None, :], 0), axis=1)
    pairs = jnp.sum(match)
    spare = index >= pairs
    pair_tile = listed(tile)
    pair_query = jnp.where(spare, owner[0] * query_tiles, listed(owner * query_tiles + slot))
    pair_out = jnp.where(
        spare, owner[0] * 2 * query_tiles, listed(owner * 2 * query_tiles + slot)
    )
    return pair_tile, pair_query, pair_out, pairs.reshape(1)


def shards(key_feats, query_feats, key_dest, key_scene, key_count, pos_tile, pos_row):
    tiles, rows, width = key_feats.shape
    query_tiles = query_feats.shape[0]
    devices = lax.axis_size("cam") * lax.axis_size("lidar")
    queries = lax.all_gather(unit_rows(query_feats), AXES, axis=0, tiled=True)

    device_iota = jnp.arange(devices, dtype=jnp.int32)
    owned = key_dest[None, :] == device_iota[:, None]
    scene_out = jnp.sum(jnp.where(owned, key_scene[None, :] + 1, 0), axis=1)
    scene_in = exchange(scene_out.reshape(devices, 1, 1)).reshape(devices)
    pos_source = pos_tile // tiles
    hit = pos_source[None, :] == device_iota[:, None]
    query_scene = jnp.sum(jnp.where(hit, scene_in[:, None], 0), axis=0)
    same = scene_in[:, None] == query_scene[None, :]
    code = jnp.where(
        hit[:, :, None], pos_row[None, :, :], jnp.where(same[:, :, None], -1, -2)
    )
    code = exchange(code)

    nk = pltpu.with_memory_space_constraint(unit_rows(key_feats), pltpu.HBM)
    pair_tile, pair_query, pair_out, pairs = pair_lists(code, key_dest, query_tiles)
    code = code.reshape(devices * query_tiles, rows)
    most = pair_tile.shape[0]
    slots = (TOTAL_AHEAD + 1) * TOTAL_GROUP
    partial, expo, picks = tile_call(
        functools.partial(total_kernel, query_tiles),
        in_space(pltpu.SMEM, [pair_tile, pair_query, pair_out, pairs, key_count])
        + in_space(pl.ANY, [nk, queries])
        + in_space(pltpu.VMEM, [code]),
        [
            jax.ShapeDtypeStruct((devices * 2 * query_tiles, rows), jnp.float32),
            pltpu.VMEM((most, rows, rows), jnp.float32),
            pltpu.VMEM((most, rows, width), jnp.bfloat16),
        ],
        [pltpu.VMEM] * 3,
        [
            pltpu.VMEM((slots, rows, width), jnp.bfloat16),
            pltpu.SemaphoreType.DMA((slots,)),
            pltpu.SemaphoreType.DMA((slots,)),
        ],
        TOTAL_MIB,
        "totals",
    )
    expo = pltpu.with_memory_space_constraint(expo, pltpu.VMEM)
    picks = pltpu.with_memory_space_constraint(picks, pltpu.VMEM)
    partial = partial.reshape(devices, 2 * query_tiles, rows)
    scale, loss = tile_call(
        share_kernel,
        in_space(pltpu.VMEM, [exchange(partial)]),
        [
            jax.ShapeDtypeStruct((devices, query_tiles, rows), jnp.float32),
            jax.ShapeDtypeStruct((query_tiles, rows), jnp.float32),
        ],
        [pltpu.VMEM] * 2,
        [],
        SHARE_MIB,
        "share",
    )
    scale = exchange(scale)
    (key_grad,) = tile_call(
        grad_kernel,
        in_space(pltpu.SMEM, [pair_tile, pair_query, pairs])
        + in_space(pltpu.VMEM, [expo, picks, code, scale.reshape(devices * query_tiles, rows)]),
        [jax.ShapeDtypeStruct((tiles, rows, width), jnp.bfloat16)],
        [pl.ANY],
        [
            pltpu.VMEM((rows, width), jnp.float32),
            pltpu.VMEM((tiles + 1, rows, width), jnp.bfloat16),
            pltpu.SemaphoreType.DMA((tiles // OUT_GROUP,)),
            pltpu.SMEM((1,), jnp.int32),
        ],
        GRAD_MIB,
        "grads",
    )
    return (loss, key_grad)


def solution(mesh):
    return jax.shard_map(
        shards,
        mesh=mesh,
        in_specs=(
            P(AXES, None, None),
            P(AXES, None, None),
            P(AXES),
            P(AXES),
            P(AXES),
            P(AXES),
            P(AXES, None),
        ),
        out_specs=(P(AXES, None), P(AXES, None, None)),
        check_vma=False,
    )
```

```python
import functools
import math

import jax
import jax.numpy as jnp
from jax import lax
from jax.experimental import pallas as pl
from jax.experimental.pallas import tpu as pltpu
from jax.sharding import PartitionSpec as P

inv_temp = 1.0 / 0.07
log2_scale = inv_temp * math.log2(math.e)
eps = 1e-06
TOTAL_GROUP = 8
TOTAL_AHEAD = 3
GRAD_GROUP = 16
OUT_GROUP = 8
TOTAL_MIB = 5
GRAD_MIB = 5
SHARE_MIB = 2
AXES = ("cam", "lidar")


def unit_rows(x):
    xf = x.astype(jnp.float32)
    scaled = (
        xf * lax.rsqrt(jnp.mean(xf * xf, axis=-1, keepdims=True) + eps) / math.sqrt(x.shape[-1])
    )
    return scaled.astype(jnp.bfloat16)


def exchange(x):
    return lax.all_to_all(x, AXES, split_axis=0, concat_axis=0, tiled=True)


def products(keys, queries):
    return lax.dot_general(
        keys, queries, (((1,), (1,)), ((), ())), preferred_element_type=jnp.float32
    )


def over_pairs(pairs, group, ahead, sources, first, body, last=None, need=None):
    groups = (pairs + (group - 1)) // group

    def fetch(step, act):
        base = lax.rem(step, ahead + 1) * group
        for j in range(group):
            p = step * group + j
            for hbm, index, buf, sem in sources:
                act(pltpu.make_async_copy(hbm.at[index[p]], buf.at[p], sem.at[base + j]))

    start = lambda copy: copy.start()
    for early in range(ahead):

        @pl.when(early < groups)
        def _():
            fetch(early, start)

    first()

    @pl.loop(0, groups)
    def _(step):
        @pl.when(step + ahead < groups)
        def _():
            fetch(step + ahead, start)

        fetch(step, lambda copy: copy.wait())
        if need is not None:
            need(step)
        for j in range(group):
            body(step * group + j)
        if last is not None:
            last(step)


def total_kernel(
    half, pair_tile, pair_query, pair_out, pairs, count, nk_hbm, q_hbm, code_ref,
    out_ref, expo_ref, q_ref, nk_buf, nk_sem, q_sem, held,
):
    row = lax.broadcasted_iota(jnp.int32, expo_ref.shape[1:], 0)

    chunks = nk_buf.shape[0] // OUT_GROUP

    def chunk(index):
        span = pl.ds(index * OUT_GROUP, OUT_GROUP)
        return pltpu.make_async_copy(nk_hbm.at[span], nk_buf.at[span], nk_sem.at[index])

    def hold_until(most):
        ready = jnp.maximum(most, held[0])

        @pl.loop(held[0], ready)
        def _(index):
            chunk(index).wait()

        held[0] = ready

    def first():
        for index in range(1, chunks):
            chunk(index).start()
        out_ref[...] = jnp.zeros_like(out_ref)

    def need(step):
        final = jnp.minimum((step + 1) * TOTAL_GROUP, pairs[0]) - 1
        hold_until(pair_tile[final] // OUT_GROUP + 1)

    held[0] = 0
    chunk(0).start()

    def body(p):
        raw = products(nk_buf[pair_tile[p]], q_ref[p])
        code = code_ref[pl.ds(pair_query[p], 1), :]
        expo = jnp.where(row < count[pair_tile[p]], jnp.exp2(raw * log2_scale), 0.0)
        expo_ref[p] = expo
        total = jnp.sum(expo, axis=0, keepdims=True)
        picked = jnp.sum(jnp.where(row == code, raw, 0.0), axis=0, keepdims=True)
        out_ref[pl.ds(pair_out[p], 1), :] = jnp.where(code > -2, total, 0.0)
        out_ref[pl.ds(pair_out[p] + half, 1), :] = picked * inv_temp

    sources = [(q_hbm, pair_query, q_ref, q_sem)]
    over_pairs(pairs[0], TOTAL_GROUP, TOTAL_AHEAD, sources, first, body, need=need)
    hold_until(chunks)


def share_kernel(arrived_ref, scale_ref, loss_ref):
    half = loss_ref.shape[0]
    sums = jnp.sum(arrived_ref[...], axis=0)
    total = sums[:half]
    loss_ref[...] = jnp.log(total) - sums[half:]
    scale_ref[...] = jnp.broadcast_to((1.0 / total)[None], scale_ref.shape)


def grad_kernel(
    pair_tile, pair_query, pairs, expo_ref, q_ref, code_ref, scale_ref, out_hbm,
    sum_buf, out_buf, out_sem, sent,
):
    row = lax.broadcasted_iota(jnp.int32, expo_ref.shape[1:], 0)
    most = pair_tile.shape[0]
    tiles = out_hbm.shape[0]

    def part(group):
        span = pl.ds(group * OUT_GROUP, OUT_GROUP)
        return pltpu.make_async_copy(out_buf.at[span], out_hbm.at[span], out_sem.at[group])

    def send_until(tile):
        ready = jnp.maximum(tile // OUT_GROUP, sent[0])

        @pl.loop(sent[0], ready)
        def _(group):
            part(group).start()

        sent[0] = ready

    def first():
        out_buf[...] = jnp.zeros_like(out_buf)
        sum_buf[...] = jnp.zeros_like(sum_buf)
        sent[0] = 0

    def body(p):
        valid = p < pairs[0]
        tile, query = pair_tile[p], pair_query[p]
        code = code_ref[pl.ds(query, 1), :]
        scale = jnp.where(code > -2, scale_ref[pl.ds(query, 1), :], 0.0)
        target = jnp.where(row == code, 1.0, 0.0)
        weights = (expo_ref[p] * scale - target).astype(jnp.bfloat16)
        grad = jnp.dot(weights, q_ref[p], preferred_element_type=jnp.float32)
        same = pair_tile[jnp.maximum(p - 1, 0)] == tile
        grad = jnp.where(same, sum_buf[...], 0.0) + grad
        sum_buf[...] = grad
        out_buf[jnp.where(valid, tile, tiles)] = (grad * inv_temp).astype(jnp.bfloat16)

    def last(step):
        ahead = (step + 1) * GRAD_GROUP
        send_until(jnp.where(ahead < pairs[0], pair_tile[jnp.minimum(ahead, most - 1)], 0))

    over_pairs(pairs[0], GRAD_GROUP, 0, [], first, body, last)
    send_until(tiles)

    @pl.loop(0, tiles // OUT_GROUP)
    def _(group):
        part(group).wait()


def tile_call(kernel, operands, out_shape, out_spaces, scratch, vmem_mib, name):
    return pl.pallas_call(
        kernel,
        in_specs=[pl.BlockSpec(memory_space=space) for space, _ in operands],
        out_specs=[pl.BlockSpec(memory_space=space) for space in out_spaces],
        out_shape=out_shape,
        scratch_shapes=scratch,
        compiler_params=pltpu.CompilerParams(vmem_limit_bytes=vmem_mib * 1024 * 1024),
        name=name,
    )(*[x for _, x in operands])


def in_space(space, arrays):
    return [(space, x) for x in arrays]


def pair_lists(code, key_dest, query_tiles):
    devices = code.shape[0]
    most = key_dest.shape[0] * query_tiles
    owned = key_dest[:, None] == jnp.arange(devices, dtype=jnp.int32)[None, :]
    allowed = (code[:, :, 0] > -2).astype(jnp.int32)
    match = jnp.sum(jnp.where(owned[:, :, None], allowed[None], 0), axis=1).reshape(most)
    index = jnp.arange(most, dtype=jnp.int32)
    place = jnp.sum(jnp.where(index[None, :] < index[:, None], match[None, :], 0), axis=1)
    tile = index // query_tiles
    slot = index % query_tiles
    owner = jnp.repeat(key_dest, query_tiles)
    chosen = (place[None, :] == index[:, None]) & (match[None, :] > 0)
    listed = lambda x: jnp.sum(jnp.where(chosen, x[None, :], 0), axis=1)
    pairs = jnp.sum(match)
    spare = index >= pairs
    pair_tile = listed(tile)
    pair_query = jnp.where(spare, owner[0] * query_tiles, listed(owner * query_tiles + slot))
    pair_out = jnp.where(
        spare, owner[0] * 2 * query_tiles, listed(owner * 2 * query_tiles + slot)
    )
    return pair_tile, pair_query, pair_out, pairs.reshape(1)


def shards(key_feats, query_feats, key_dest, key_scene, key_count, pos_tile, pos_row):
    tiles, rows, width = key_feats.shape
    query_tiles = query_feats.shape[0]
    devices = lax.axis_size("cam") * lax.axis_size("lidar")
    queries = lax.all_gather(unit_rows(query_feats), AXES, axis=0, tiled=True)

    device_iota = jnp.arange(devices, dtype=jnp.int32)
    owned = key_dest[None, :] == device_iota[:, None]
    scene_out = jnp.sum(jnp.where(owned, key_scene[None, :] + 1, 0), axis=1)
    scene_in = exchange(scene_out.reshape(devices, 1, 1)).reshape(devices)
    pos_source = pos_tile // tiles
    hit = pos_source[None, :] == device_iota[:, None]
    query_scene = jnp.sum(jnp.where(hit, scene_in[:, None], 0), axis=0)
    same = scene_in[:, None] == query_scene[None, :]
    code = jnp.where(
        hit[:, :, None], pos_row[None, :, :], jnp.where(same[:, :, None], -1, -2)
    )
    code = exchange(code)

    nk = pltpu.with_memory_space_constraint(unit_rows(key_feats), pltpu.HBM)
    pair_tile, pair_query, pair_out, pairs = pair_lists(code, key_dest, query_tiles)
    code = code.reshape(devices * query_tiles, rows)
    most = pair_tile.shape[0]
    slots = (TOTAL_AHEAD + 1) * TOTAL_GROUP
    partial, expo, picks = tile_call(
        functools.partial(total_kernel, query_tiles),
        in_space(pltpu.SMEM, [pair_tile, pair_query, pair_out, pairs, key_count])
        + in_space(pl.ANY, [nk, queries])
        + in_space(pltpu.VMEM, [code]),
        [
            jax.ShapeDtypeStruct((devices * 2 * query_tiles, rows), jnp.float32),
            pltpu.VMEM((most, rows, rows), jnp.float32),
            pltpu.VMEM((most, rows, width), jnp.bfloat16),
        ],
        [pltpu.VMEM] * 3,
        [
            pltpu.VMEM((tiles, rows, width), jnp.bfloat16),
            pltpu.SemaphoreType.DMA((tiles // OUT_GROUP,)),
            pltpu.SemaphoreType.DMA((slots,)),
            pltpu.SMEM((1,), jnp.int32),
        ],
        TOTAL_MIB,
        "totals",
    )
    expo = pltpu.with_memory_space_constraint(expo, pltpu.VMEM)
    picks = pltpu.with_memory_space_constraint(picks, pltpu.VMEM)
    partial = partial.reshape(devices, 2 * query_tiles, rows)
    scale, loss = tile_call(
        share_kernel,
        in_space(pltpu.VMEM, [exchange(partial)]),
        [
            jax.ShapeDtypeStruct((devices, query_tiles, rows), jnp.float32),
            jax.ShapeDtypeStruct((query_tiles, rows), jnp.float32),
        ],
        [pltpu.VMEM] * 2,
        [],
        SHARE_MIB,
        "share",
    )
    scale = exchange(scale)
    (key_grad,) = tile_call(
        grad_kernel,
        in_space(pltpu.SMEM, [pair_tile, pair_query, pairs])
        + in_space(pltpu.VMEM, [expo, picks, code, scale.reshape(devices * query_tiles, rows)]),
        [jax.ShapeDtypeStruct((tiles, rows, width), jnp.bfloat16)],
        [pl.ANY],
        [
            pltpu.VMEM((rows, width), jnp.float32),
            pltpu.VMEM((tiles + 1, rows, width), jnp.bfloat16),
            pltpu.SemaphoreType.DMA((tiles // OUT_GROUP,)),
            pltpu.SMEM((1,), jnp.int32),
        ],
        GRAD_MIB,
        "grads",
    )
    return (loss, key_grad)


def solution(mesh):
    return jax.shard_map(
        shards,
        mesh=mesh,
        in_specs=(
            P(AXES, None, None),
            P(AXES, None, None),
            P(AXES),
            P(AXES),
            P(AXES),
            P(AXES),
            P(AXES, None),
        ),
        out_specs=(P(AXES, None), P(AXES, None, None)),
        check_vma=False,
    )
```

```python
import functools
import math

import jax
import jax.numpy as jnp
from jax import lax
from jax.experimental import pallas as pl
from jax.experimental.pallas import tpu as pltpu
from jax.sharding import PartitionSpec as P

inv_temp = 1.0 / 0.07
log2_scale = inv_temp * math.log2(math.e)
eps = 1e-06
TOTAL_GROUP = 16
TOTAL_AHEAD = 2
GRAD_GROUP = 16
OUT_GROUP = 8
TOTAL_MIB = 5
GRAD_MIB = 5
SHARE_MIB = 2
AXES = ("cam", "lidar")


def unit_rows(x):
    xf = x.astype(jnp.float32)
    scaled = (
        xf * lax.rsqrt(jnp.mean(xf * xf, axis=-1, keepdims=True) + eps) / math.sqrt(x.shape[-1])
    )
    return scaled.astype(jnp.bfloat16)


def exchange(x):
    return lax.all_to_all(x, AXES, split_axis=0, concat_axis=0, tiled=True)


def products(keys, queries):
    return lax.dot_general(
        keys, queries, (((1,), (1,)), ((), ())), preferred_element_type=jnp.float32
    )


def over_pairs(pairs, group, ahead, sources, first, body, last=None, need=None):
    groups = (pairs + (group - 1)) // group

    def fetch(step, act):
        base = lax.rem(step, ahead + 1) * group
        for j in range(group):
            p = step * group + j
            for hbm, index, buf, sem in sources:
                act(pltpu.make_async_copy(hbm.at[index[p]], buf.at[p], sem.at[base + j]))

    start = lambda copy: copy.start()
    for early in range(ahead):

        @pl.when(early < groups)
        def _():
            fetch(early, start)

    first()

    @pl.loop(0, groups)
    def _(step):
        @pl.when(step + ahead < groups)
        def _():
            fetch(step + ahead, start)

        fetch(step, lambda copy: copy.wait())
        if need is not None:
            need(step)
        for j in range(group):
            body(step * group + j)
        if last is not None:
            last(step)


def total_kernel(
    half, pair_tile, pair_query, pair_out, pairs, count, nk_hbm, q_hbm, code_ref,
    out_ref, expo_ref, q_ref, nk_buf, nk_sem, q_sem, held,
):
    row = lax.broadcasted_iota(jnp.int32, expo_ref.shape[1:], 0)

    chunks = nk_buf.shape[0] // OUT_GROUP

    def chunk(index):
        span = pl.ds(index * OUT_GROUP, OUT_GROUP)
        return pltpu.make_async_copy(nk_hbm.at[span], nk_buf.at[span], nk_sem.at[index])

    def hold_until(most):
        ready = jnp.maximum(most, held[0])

        @pl.loop(held[0], ready)
        def _(index):
            chunk(index).wait()

        held[0] = ready

    def first():
        for index in range(1, chunks):
            chunk(index).start()
        out_ref[...] = jnp.zeros_like(out_ref)

    def need(step):
        final = jnp.minimum((step + 1) * TOTAL_GROUP, pairs[0]) - 1
        hold_until(pair_tile[final] // OUT_GROUP + 1)

    held[0] = 0
    chunk(0).start()

    def body(p):
        raw = products(nk_buf[pair_tile[p]], q_ref[p])
        code = code_ref[pl.ds(pair_query[p], 1), :]
        expo = jnp.where(row < count[pair_tile[p]], jnp.exp2(raw * log2_scale), 0.0)
        expo_ref[p] = expo
        total = jnp.sum(expo, axis=0, keepdims=True)
        picked = jnp.sum(jnp.where(row == code, raw, 0.0), axis=0, keepdims=True)
        out_ref[pl.ds(pair_out[p], 1), :] = jnp.where(code > -2, total, 0.0)
        out_ref[pl.ds(pair_out[p] + half, 1), :] = picked * inv_temp

    sources = [(q_hbm, pair_query, q_ref, q_sem)]
    over_pairs(pairs[0], TOTAL_GROUP, TOTAL_AHEAD, sources, first, body, need=need)
    hold_until(chunks)


def share_kernel(arrived_ref, scale_ref, loss_ref):
    half = loss_ref.shape[0]
    sums = jnp.sum(arrived_ref[...], axis=0)
    total = sums[:half]
    loss_ref[...] = jnp.log(total) - sums[half:]
    scale_ref[...] = jnp.broadcast_to((1.0 / total)[None], scale_ref.shape)


def grad_kernel(
    pair_tile, pair_query, pairs, expo_ref, q_ref, code_ref, scale_ref, out_hbm,
    sum_buf, out_buf, out_sem, sent,
):
    row = lax.broadcasted_iota(jnp.int32, expo_ref.shape[1:], 0)
    most = pair_tile.shape[0]
    tiles = out_hbm.shape[0]

    def part(group):
        span = pl.ds(group * OUT_GROUP, OUT_GROUP)
        return pltpu.make_async_copy(out_buf.at[span], out_hbm.at[span], out_sem.at[group])

    def send_until(tile):
        ready = jnp.maximum(tile // OUT_GROUP, sent[0])

        @pl.loop(sent[0], ready)
        def _(group):
            part(group).start()

        sent[0] = ready

    def first():
        out_buf[...] = jnp.zeros_like(out_buf)
        sum_buf[...] = jnp.zeros_like(sum_buf)
        sent[0] = 0

    def body(p):
        valid = p < pairs[0]
        tile, query = pair_tile[p], pair_query[p]
        code = code_ref[pl.ds(query, 1), :]
        scale = jnp.where(code > -2, scale_ref[pl.ds(query, 1), :], 0.0)
        target = jnp.where(row == code, 1.0, 0.0)
        weights = (expo_ref[p] * scale - target).astype(jnp.bfloat16)
        grad = jnp.dot(weights, q_ref[p], preferred_element_type=jnp.float32)
        same = pair_tile[jnp.maximum(p - 1, 0)] == tile
        grad = jnp.where(same, sum_buf[...], 0.0) + grad
        sum_buf[...] = grad
        out_buf[jnp.where(valid, tile, tiles)] = (grad * inv_temp).astype(jnp.bfloat16)

    def last(step):
        ahead = (step + 1) * GRAD_GROUP
        send_until(jnp.where(ahead < pairs[0], pair_tile[jnp.minimum(ahead, most - 1)], 0))

    over_pairs(pairs[0], GRAD_GROUP, 0, [], first, body, last)
    send_until(tiles)

    @pl.loop(0, tiles // OUT_GROUP)
    def _(group):
        part(group).wait()


def tile_call(kernel, operands, out_shape, out_spaces, scratch, vmem_mib, name):
    return pl.pallas_call(
        kernel,
        in_specs=[pl.BlockSpec(memory_space=space) for space, _ in operands],
        out_specs=[pl.BlockSpec(memory_space=space) for space in out_spaces],
        out_shape=out_shape,
        scratch_shapes=scratch,
        compiler_params=pltpu.CompilerParams(vmem_limit_bytes=vmem_mib * 1024 * 1024),
        name=name,
    )(*[x for _, x in operands])


def in_space(space, arrays):
    return [(space, x) for x in arrays]


def pair_lists(code, key_dest, query_tiles):
    devices = code.shape[0]
    most = key_dest.shape[0] * query_tiles
    owned = key_dest[:, None] == jnp.arange(devices, dtype=jnp.int32)[None, :]
    allowed = (code[:, :, 0] > -2).astype(jnp.int32)
    match = jnp.sum(jnp.where(owned[:, :, None], allowed[None], 0), axis=1).reshape(most)
    index = jnp.arange(most, dtype=jnp.int32)
    place = jnp.sum(jnp.where(index[None, :] < index[:, None], match[None, :], 0), axis=1)
    tile = index // query_tiles
    slot = index % query_tiles
    owner = jnp.repeat(key_dest, query_tiles)
    chosen = (place[None, :] == index[:, None]) & (match[None, :] > 0)
    listed = lambda x: jnp.sum(jnp.where(chosen, x[None, :], 0), axis=1)
    pairs = jnp.sum(match)
    spare = index >= pairs
    pair_tile = listed(tile)
    pair_query = jnp.where(spare, owner[0] * query_tiles, listed(owner * query_tiles + slot))
    pair_out = jnp.where(
        spare, owner[0] * 2 * query_tiles, listed(owner * 2 * query_tiles + slot)
    )
    return pair_tile, pair_query, pair_out, pairs.reshape(1)


def shards(key_feats, query_feats, key_dest, key_scene, key_count, pos_tile, pos_row):
    tiles, rows, width = key_feats.shape
    query_tiles = query_feats.shape[0]
    devices = lax.axis_size("cam") * lax.axis_size("lidar")
    queries = lax.all_gather(unit_rows(query_feats), AXES, axis=0, tiled=True)

    device_iota = jnp.arange(devices, dtype=jnp.int32)
    owned = key_dest[None, :] == device_iota[:, None]
    scene_out = jnp.sum(jnp.where(owned, key_scene[None, :] + 1, 0), axis=1)
    scene_in = exchange(scene_out.reshape(devices, 1, 1)).reshape(devices)
    pos_source = pos_tile // tiles
    hit = pos_source[None, :] == device_iota[:, None]
    query_scene = jnp.sum(jnp.where(hit, scene_in[:, None], 0), axis=0)
    same = scene_in[:, None] == query_scene[None, :]
    code = jnp.where(
        hit[:, :, None], pos_row[None, :, :], jnp.where(same[:, :, None], -1, -2)
    )
    code = exchange(code)

    nk = pltpu.with_memory_space_constraint(unit_rows(key_feats), pltpu.HBM)
    pair_tile, pair_query, pair_out, pairs = pair_lists(code, key_dest, query_tiles)
    code = code.reshape(devices * query_tiles, rows)
    most = pair_tile.shape[0]
    slots = (TOTAL_AHEAD + 1) * TOTAL_GROUP
    partial, expo, picks = tile_call(
        functools.partial(total_kernel, query_tiles),
        in_space(pltpu.SMEM, [pair_tile, pair_query, pair_out, pairs, key_count])
        + in_space(pl.ANY, [nk, queries])
        + in_space(pltpu.VMEM, [code]),
        [
            jax.ShapeDtypeStruct((devices * 2 * query_tiles, rows), jnp.float32),
            pltpu.VMEM((most, rows, rows), jnp.float32),
            pltpu.VMEM((most, rows, width), jnp.bfloat16),
        ],
        [pltpu.VMEM] * 3,
        [
            pltpu.VMEM((tiles, rows, width), jnp.bfloat16),
            pltpu.SemaphoreType.DMA((tiles // OUT_GROUP,)),
            pltpu.SemaphoreType.DMA((slots,)),
            pltpu.SMEM((1,), jnp.int32),
        ],
        TOTAL_MIB,
        "totals",
    )
    expo = pltpu.with_memory_space_constraint(expo, pltpu.VMEM)
    picks = pltpu.with_memory_space_constraint(picks, pltpu.VMEM)
    partial = partial.reshape(devices, 2 * query_tiles, rows)
    scale, loss = tile_call(
        share_kernel,
        in_space(pltpu.VMEM, [exchange(partial)]),
        [
            jax.ShapeDtypeStruct((devices, query_tiles, rows), jnp.float32),
            jax.ShapeDtypeStruct((query_tiles, rows), jnp.float32),
        ],
        [pltpu.VMEM] * 2,
        [],
        SHARE_MIB,
        "share",
    )
    scale = exchange(scale)
    (key_grad,) = tile_call(
        grad_kernel,
        in_space(pltpu.SMEM, [pair_tile, pair_query, pairs])
        + in_space(pltpu.VMEM, [expo, picks, code, scale.reshape(devices * query_tiles, rows)]),
        [jax.ShapeDtypeStruct((tiles, rows, width), jnp.bfloat16)],
        [pl.ANY],
        [
            pltpu.VMEM((rows, width), jnp.float32),
            pltpu.VMEM((tiles + 1, rows, width), jnp.bfloat16),
            pltpu.SemaphoreType.DMA((tiles // OUT_GROUP,)),
            pltpu.SMEM((1,), jnp.int32),
        ],
        GRAD_MIB,
        "grads",
    )
    return (loss, key_grad)


def solution(mesh):
    return jax.shard_map(
        shards,
        mesh=mesh,
        in_specs=(
            P(AXES, None, None),
            P(AXES, None, None),
            P(AXES),
            P(AXES),
            P(AXES),
            P(AXES),
            P(AXES, None),
        ),
        out_specs=(P(AXES, None), P(AXES, None, None)),
        check_vma=False,
    )
```
